512 devices in a mesh: expert: 64 (over x, y, core), hsplit: 8 (over z).
Axes of the slice: x: 4, y: 8, z: 8, core: 2. Of those that a mesh axis runs over, the one named last changes fastest.
Arguments:
- tokens: bfloat16 [1024, 7168], P('expert'), may hold values from -6 to 6
- routes: int32 [1024, 8], P('expert'), may hold values from 0 to 15, all different within a row; in each aligned block of 4 rows (0 to 3, 4 to 7, ...) at most 4 rows name the same one
- route_weights: float32 [1024, 8], P('expert'), may hold values from 0.05 to 0.6
- gate_weight: bfloat16 [64, 1792, 2048], P('expert', None, 'hsplit'), may hold values from -0.0625 to 0.0625
- up_weight: bfloat16 [64, 1792, 2048], P('expert', None, 'hsplit'), may hold values from -0.0625 to 0.0625
- down_weight: bfloat16 [64, 2048, 1792], P('expert', 'hsplit'), may hold values from -0.125 to 0.125
Outputs:
- routed_out: bfloat16 [1024, 7168], P('expert', 'hsplit')
The draws below stay inside these ranges and needn't reach their ends.
Inputs may be any that keep to these rules, and one draw needn't show every extreme that they name: `routes`: each token names 8 different experts. In each aligned block of 4 tokens (one of 4 blocks of the tokens of one index of the expert axis) some expert is named by every token of the block.
All inputs are finite; a program needn't handle non-finite values.
Results may differ from the reference program's by a relative error of at most 0.02.
Values may be sent and summed in bfloat16 or wider, within the bound.
A program may use at most 128 MiB of HBM per device.

```python
import math
import jax
import jax.numpy as jnp
import numpy as np
from jax import lax

D = 7168
FF = 2048
TOP = 8
EXPERTS = 16
GROUP = 4
MOST = 4
TOKENS = 1024
N_EXPERT = 64
N_HSPLIT = 8


def level_of(rng, shape, shards, smallest, top_value):
    def one(axis_at, blocks):
        steps = jax.random.uniform(jax.random.fold_in(jax.random.fold_in(rng, 6), axis_at), (blocks,), jnp.float32, smallest / len(shards), top_value / len(shards))
        return jnp.repeat(jnp.exp(steps), shape[axis_at] // blocks).reshape((-1,) + (1,) * (len(shape) - axis_at - 1))

    level = one(*shards[0])
    for cut in shards[1:]:
        level = level * one(*cut)
    return level


def deal_out(key, own, number, rows, amount, top, limit, skew):
    order = jax.random.permutation(key, amount)
    heavy_load, usual = load_shares(amount, rows * top, limit, skew, True), load_shares(amount, rows * top, limit, skew, False)
    places = jnp.arange(amount)

    def named(sizes, rotation):
        used = int((sizes > 0).sum())
        fixed = max(1, used // 4)
        shifted = fixed + (places - fixed + rotation * (used - fixed)) % max(1, amount - fixed)
        return jnp.zeros((amount,), jnp.int32).at[order[jnp.where(places < fixed, places, shifted)]].set(jnp.asarray(sizes, jnp.int32))

    sizes = jnp.where(number % 4 == 0, named(heavy_load, number // 4), named(usual, number - number // 4 - 1))
    mixed = jax.random.permutation(jax.random.fold_in(own, 3), amount)
    donor, taker = mixed[0:amount // 2 * 2:2], mixed[1:amount // 2 * 2:2]
    slack = jnp.minimum(sizes[donor] - 1, limit - sizes[taker]) // 2
    slack = jnp.where((donor == order[0]) | (taker == order[0]) | (sizes[taker] == 0), 0, jnp.maximum(slack, 0))
    shifted = jax.random.randint(jax.random.fold_in(own, 4), (amount // 2,), 0, 1 << 20) % (slack + 1)
    sizes = sizes.at[donor].add(-shifted).at[taker].add(shifted)
    members = jnp.searchsorted(jnp.cumsum(sizes), jnp.arange(rows * top), side="right").astype(jnp.int32)
    grid = members.reshape(top, rows).T
    grid = grid[jax.random.permutation(jax.random.fold_in(own, 1), rows)]
    rotation = jax.random.randint(jax.random.fold_in(own, 2), (rows, 1), 0, top)
    return jnp.take_along_axis(grid, (jnp.arange(top)[None, :] + rotation) % top, axis=1)


def load_shares(amount, total, reach, skew, full):
    weights = [(1 << 20) // math.isqrt(standing ** skew) + 1 for standing in range(1, amount + 1)]
    largest = reach if full else min(reach, max(-(-total // amount), total * weights[0] // sum(weights)))
    least = 1 if total - largest >= amount - 1 else 0
    counts, spare = [largest] + [least] * (amount - 1), total - largest - least * (amount - 1)
    while spare > 0:
        free = [i for i in range(1, amount) if counts[i] < largest] or [i for i in range(1, amount) if counts[i] < reach]
        whole, remaining = sum([weights[i] for i in free]), spare
        for i in free:
            more = min(reach - counts[i], max(1, remaining * weights[i] // whole), spare)
            counts[i] = counts[i] + more
            spare = spare - more
    return np.array(counts)


def bell_draw(key, dims, width, bound, pieces=(), held_as=jnp.bfloat16):
    loudness = level_of(key, dims, pieces, -0.22, 0.18) if pieces else 1.0
    drawn = jax.random.normal(key, dims, jnp.float32) * width * loudness
    return jnp.minimum(jnp.maximum(drawn, -bound), bound).astype(held_as)


def setup_inputs(seed: int = 0) -> dict:
    seeds = jax.random.split(jax.random.key(seed), 7)
    tokens = bell_draw(seeds[0], (TOKENS, D), 1.0, 6.0, ((0, 64),))
    routes_keys = jax.random.split(jax.random.fold_in(seeds[1], 1), TOKENS // MOST)
    routes_turns = jax.random.permutation(jax.random.fold_in(seeds[1], 3), TOKENS // MOST)
    routes = jax.vmap(lambda own, number: deal_out(jax.random.fold_in(seeds[1], 2), own, number, MOST, EXPERTS, TOP, MOST, 2))(routes_keys, routes_turns).reshape((TOKENS, TOP))
    route_weights = jnp.clip(0.05 + 0.55 * jax.random.uniform(seeds[2], (TOKENS, TOP), jnp.float32) ** level_of(seeds[2], (TOKENS, TOP), ((0, 64),), -0.2, 0.2), 0.05, 0.6)
    gate_weight = bell_draw(seeds[3], (N_EXPERT, D // GROUP, FF), D ** -0.5, 0.0625, ((0, 64), (2, 8)))
    up_weight = bell_draw(seeds[4], (N_EXPERT, D // GROUP, FF), D ** -0.5, 0.0625, ((0, 64), (2, 8)))
    down_weight = bell_draw(seeds[5], (N_EXPERT, FF, D // GROUP), FF ** -0.5, 0.125, ((0, 64), (1, 8)))
    return dict(tokens=tokens, routes=routes, route_weights=route_weights, gate_weight=gate_weight, up_weight=up_weight, down_weight=down_weight)


def reference(tokens, routes, route_weights, gate_weight, up_weight, down_weight):
    model_width = tokens.shape[1]
    piece_width = model_width // (GROUP * N_HSPLIT)
    gate_all = gate_weight.reshape(EXPERTS, model_width, FF)
    up_all = up_weight.reshape(EXPERTS, model_width, FF)
    down_all = down_weight.reshape(EXPERTS, GROUP, FF, N_HSPLIT, piece_width).transpose(0, 2, 3, 1, 4).reshape(EXPERTS, FF, model_width)
    capacity = GROUP * N_EXPERT * MOST
    token_ids = jnp.broadcast_to(jnp.arange(TOKENS, dtype=jnp.int32)[:, None], (TOKENS, TOP)).reshape(-1)
    flat_routes = routes.reshape(-1)
    flat_weights = route_weights.reshape(-1)

    def one_expert(running, packed):
        expert_id, w_gate, w_up, w_down = packed
        hits = flat_routes == expert_id
        ranking = jnp.cumsum(hits.astype(jnp.int32)) - 1
        target = jnp.where(hits, ranking, capacity).astype(jnp.int32)
        chosen = jnp.zeros((capacity,), jnp.int32).at[target].set(token_ids, mode="drop")
        factor = jnp.zeros((capacity,), jnp.float32).at[target].set(flat_weights, mode="drop")
        picked = tokens[chosen]
        gate_value = jnp.dot(picked, w_gate, preferred_element_type=jnp.float32)
        up_value = jnp.dot(picked, w_up, preferred_element_type=jnp.float32)
        hidden = lax.optimization_barrier((jax.nn.silu(gate_value) * up_value).astype(jnp.bfloat16))
        shares = hidden.reshape(capacity, N_HSPLIT, FF // N_HSPLIT).transpose(1, 0, 2).astype(jnp.float32)
        down_parts = w_down.reshape(N_HSPLIT, FF // N_HSPLIT, model_width).astype(jnp.float32)
        partial_value = jnp.einsum("hcf,hfd->hcd", shares, down_parts)
        partial_value = lax.optimization_barrier(partial_value.astype(jnp.bfloat16))
        expert_out = jnp.sum(partial_value.astype(jnp.float32), axis=0)
        expert_out = lax.optimization_barrier(expert_out.astype(jnp.bfloat16))
        running = running.at[chosen].add(factor[:, None] * expert_out.astype(jnp.float32))
        return running, None

    start_value = jnp.zeros((TOKENS, model_width), jnp.float32)
    running, _ = lax.scan(one_expert, start_value, (jnp.arange(EXPERTS, dtype=jnp.int32), gate_all, up_all, down_all))
    return running.astype(jnp.bfloat16)
```

```python
import jax
import jax.numpy as jnp
from jax import lax
from jax.sharding import PartitionSpec as P

EXPERTS = 16


def local(tokens, routes, route_weights, gate_weight, up_weight, down_weight):
    tok_dev, model_width = tokens.shape
    owners = lax.axis_size("expert")
    splits = lax.axis_size("hsplit")
    group_size = owners // EXPERTS
    slice_width = model_width // group_size
    piece_width = slice_width // splits
    units = gate_weight.shape[2]
    h = lax.axis_index("hsplit")
    groups = [[e * group_size + q for q in range(group_size)] for e in range(EXPERTS)]

    mine = lax.dynamic_slice_in_dim(
        tokens.reshape(tok_dev, group_size, splits, piece_width), h, 1, axis=2
    ).reshape(tok_dev, group_size, piece_width)
    outgoing = jnp.broadcast_to(
        mine.transpose(1, 0, 2)[None], (EXPERTS, group_size, tok_dev, piece_width)
    ).reshape(owners, tok_dev, piece_width)
    arrived = lax.all_to_all(outgoing, "expert", split_axis=0, concat_axis=0, tiled=True)
    arrived = arrived.reshape(owners * tok_dev, piece_width)
    gathered = lax.all_gather(arrived, "hsplit", axis=0)
    both = jnp.concatenate([gate_weight[0], up_weight[0]], axis=1)
    part = sum(
        jnp.dot(
            gathered[s],
            both[s * piece_width : (s + 1) * piece_width],
            preferred_element_type=jnp.float32,
        )
        for s in range(splits)
    )
    total = lax.psum_scatter(
        part.astype(jnp.bfloat16), "expert", scatter_dimension=0, tiled=True, axis_index_groups=groups
    ).astype(jnp.float32)
    hidden = (jax.nn.silu(total[:, :units]) * total[:, units:]).astype(jnp.bfloat16)
    hidden = lax.all_gather(hidden, "expert", axis=0, tiled=True, axis_index_groups=groups)
    partial = jnp.stack(
        [
            jnp.dot(
                hidden,
                down_weight[0][:, s * piece_width : (s + 1) * piece_width],
                preferred_element_type=jnp.float32,
            ).astype(jnp.bfloat16)
            for s in range(splits)
        ]
    )
    summed = lax.psum_scatter(partial, "hsplit", scatter_dimension=0, tiled=False)
    results = summed.reshape(owners, tok_dev, piece_width)
    returned = lax.all_to_all(results, "expert", split_axis=0, concat_axis=0, tiled=True)
    chosen = routes[:, :, None] == jnp.arange(EXPERTS, dtype=jnp.int32)[None, None, :]
    factor = jnp.sum(jnp.where(chosen, route_weights[:, :, None], 0.0), axis=1)
    blocks = returned.reshape(EXPERTS, group_size, tok_dev, piece_width).astype(jnp.float32)
    out = jnp.sum(blocks * factor.T[:, None, :, None], axis=0)
    return out.transpose(1, 0, 2).reshape(tok_dev, group_size * piece_width).astype(jnp.bfloat16)


def solution(mesh):
    placed = (
        P("expert", None),
        P("expert", None),
        P("expert", None),
        P("expert", None, "hsplit"),
        P("expert", None, "hsplit"),
        P("expert", "hsplit", None),
    )
    return jax.shard_map(
        local, mesh=mesh, in_specs=placed, out_specs=P("expert", "hsplit"), check_vma=False
    )
```

```python
import jax
import jax.numpy as jnp
from jax import lax
from jax.experimental import pallas as pl
from jax.experimental.pallas import tpu as pltpu
from jax.sharding import PartitionSpec as P

EXPERTS = 16
Q = 4
Z = 8
LX = 4
LY = 4
TOK = 16
D = 7168
W = D // Q
HALF = W // 2
PIECE = W // Z
UNITS = 256
ROWS = EXPERTS * TOK
SUB = ROWS // 2
SHARE = ROWS // Q
BF = jnp.bfloat16
F32 = jnp.float32


def kernel(
    tok, routes, rw, gate_in, up_in, down_in, out,
    xb, wg, wu, wd, dj, acc, pbuf, prec, hid, rsend, rrecv, fin, ret,
    w_sem, g_send, g_recv, y_send, y_recv, x_send, x_recv,
    up_send, up_recv, dn_send, dn_recv,
    p_send, p_recv, h_send, h_recv, rs_send, rs_recv, a_send, a_recv,
):
    p = lax.axis_index("expert")
    z = lax.axis_index("hsplit")
    e, q = p // Q, p % Q
    ex, ey = e // LY, e % LY
    z_up, z_dn = (z + 1) % Z, (z + Z - 1) % Z
    open_sends = []

    def remote(src, dst, send, recv, to_p, to_z):
        return pltpu.make_async_remote_copy(
            src_ref=src, dst_ref=dst, send_sem=send, recv_sem=recv,
            device_id=(to_p, to_z), device_id_type=pl.DeviceIdType.MESH,
        )

    def send(*args):
        copy = remote(*args)
        copy.start()
        open_sends.append(copy)

    def arrived(ref, sem):
        pltpu.make_async_copy(ref, ref, sem).wait()

    loads = [
        pltpu.make_async_copy(src, dst, w_sem.at[i])
        for i, (src, dst) in enumerate(((gate_in, wg), (up_in, wu), (down_in, wd)))
    ]
    for load in loads:
        load.start()

    barrier = pltpu.get_barrier_semaphore()

    def greet(i, carry):
        pl.semaphore_signal(
            barrier, inc=1, device_id=((p + i) % (EXPERTS * Q), z), device_id_type=pl.DeviceIdType.MESH
        )
        return carry

    lax.fori_loop(1, EXPERTS * Q, greet, 0)
    for to_z in (z_up, z_dn):
        pl.semaphore_signal(barrier, inc=1, device_id=(p, to_z), device_id_type=pl.DeviceIdType.MESH)
    pl.semaphore_wait(barrier, EXPERTS * Q + 1)

    mine = xb.at[z, pl.ds(pl.multiple_of(e * TOK, TOK), TOK)]
    shares = q == z // 2

    def share_of(to_q):
        start = pl.multiple_of(to_q * W + (z % 2) * HALF, 128)
        return tok.at[:, pl.ds(start, HALF)]

    g_copies = [
        remote(share_of((q + d) % Q), mine, g_send.at[d - 1], g_recv.at[0], e * Q + (q + d) % Q, z)
        for d in range(1, Q)
    ]
    own_share = pltpu.make_async_copy(share_of(q), mine, g_recv.at[0])

    @pl.when(shares)
    def _():
        for copy in g_copies:
            copy.start()
        own_share.start()

    arrived(mine, g_recv.at[0])
    for d in range(1, LY):
        send(mine, mine, y_send.at[d - 1], y_recv.at[d - 1], (ex * LY + (ey + d) % LY) * Q + q, z)
    for d in range(1, LY):
        arrived(xb.at[z, pl.ds(pl.multiple_of((ex * LY + (ey + LY - d) % LY) * TOK, TOK), TOK)], y_recv.at[d - 1])
    column = LY * TOK
    mine_x = xb.at[z, pl.ds(pl.multiple_of(ex * column, column), column)]
    for d in range(1, LX):
        send(mine_x, mine_x, x_send.at[d - 1], x_recv.at[d - 1], (((ex + d) % LX) * LY + ey) * Q + q, z)
    for load in loads:
        load.wait()
    for d in range(1, LX):
        arrived(
            xb.at[z, pl.ds(pl.multiple_of(((ex + LX - d) % LX) * column, column), column)], x_recv.at[d - 1]
        )

    steps = 7

    def half_of(block, k, way):
        which = k % 2 if way > 0 else (k + 1) % 2
        return xb.at[block, pl.ds(which * SUB, SUB)]

    def ring_send(k, way):
        block = (z - way * (k // 2) + Z) % Z
        ref = half_of(block, k, way)
        if way > 0:
            send(ref, ref, up_send.at[k], up_recv.at[k], p, z_up)
        else:
            send(ref, ref, dn_send.at[k], dn_recv.at[k], p, z_dn)

    def ring_arrived(k, way):
        block = (z - way * (k // 2 + 1) + 2 * Z) % Z
        arrived(half_of(block, k, way), (up_recv if way > 0 else dn_recv).at[k])

    def gate_up(block):
        rows = pl.ds(pl.multiple_of((block % 2) * HALF, 128), HALF)
        x = xb[block]
        return (
            jnp.dot(x, wg[rows, :], preferred_element_type=F32),
            jnp.dot(x, wu[rows, :], preferred_element_type=F32),
        )

    def add_block(block, first):
        a, b = gate_up(block)
        group = block // 2
        if first:
            acc[group, :, :UNITS] = a
            acc[group, :, UNITS:] = b
        else:
            acc[group, :, :UNITS] += a
            acc[group, :, UNITS:] += b

    side = jnp.where(z % 2 == 1, 1, Q - 1)
    own_group = z // 2
    order = (own_group, (own_group + side) % Q, (own_group + 2 * Q - side) % Q, (own_group + 2) % Q)

    def share_partials(i):
        pbuf[i] = acc[order[i]].astype(BF)
        for d in range(1, Q):
            to = (q + d) % Q
            rows = pl.ds(pl.multiple_of(to * SHARE, SHARE), SHARE)
            send(pbuf.at[i, rows], prec.at[i, d - 1], p_send.at[i, d - 1], p_recv.at[i, d - 1], e * Q + to, z)

    def share_hidden(i):
        rows = pl.ds(pl.multiple_of(q * SHARE, SHARE), SHARE)
        total = acc[order[i], rows, :]
        for d in range(1, Q):
            arrived(prec.at[i, d - 1], p_recv.at[i, d - 1])
            total += prec[i, d - 1].astype(F32)
        g, u = total[:, :UNITS], total[:, UNITS:]
        hid[order[i], rows, :] = (g / (1.0 + jnp.exp(-g)) * u).astype(BF)
        ref = hid.at[order[i], rows]
        for d in range(1, Q):
            send(ref, ref, h_send.at[i, d - 1], h_recv.at[i, d - 1], e * Q + (q + d) % Q, z)

    for k in (0, 1):
        ring_send(k, 1)
        ring_send(k, -1)
    add_block(z, True)
    for j in range(Z):
        dj[j] = wd[:, j * PIECE : (j + 1) * PIECE]
    for k in range(steps):
        for way in (1, -1):
            ring_arrived(k, way)
            if k + 2 < steps:
                ring_send(k + 2, way)
        if k == 1:
            partner = jnp.where(z % 2 == 0, z_up, z_dn)
            other = jnp.where(z % 2 == 0, z_dn, z_up)
            add_block(partner, False)
            share_partials(0)
            add_block(other, True)
        elif k == 3:
            closing = jnp.where(z % 2 == 0, (z + Z - 2) % Z, (z + 2) % Z)
            opening = jnp.where(z % 2 == 0, (z + 2) % Z, (z + Z - 2) % Z)
            add_block(closing, False)
            share_partials(1)
            share_hidden(0)
            add_block(opening, True)
        elif k == 5:
            closing = jnp.where(z % 2 == 0, (z + 3) % Z, (z + Z - 3) % Z)
            opening = jnp.where(z % 2 == 0, (z + Z - 3) % Z, (z + 3) % Z)
            add_block(closing, False)
            share_partials(2)
            share_hidden(1)
            add_block(opening, True)
            share_hidden(2)
    add_block((z + 4) % Z, False)
    share_partials(3)
    share_hidden(3)
    for i in range(Q):
        for d in range(1, Q):
            rows = pl.ds(pl.multiple_of(((q + Q - d) % Q) * SHARE, SHARE), SHARE)
            arrived(hid.at[order[i], rows], h_recv.at[i, d - 1])

    def way_of(c):
        return 1 if c < 2 else -1

    def sum_copy(c, s):
        return remote(
            rsend.at[c, s], rrecv.at[c, s], rs_send.at[c, s], rs_recv.at[c, s],
            p, z_up if way_of(c) > 0 else z_dn,
        )

    def term(c, j):
        return jnp.dot(hid[c], dj[j], preferred_element_type=F32)

    for c in (0, 2, 1, 3):
        rsend[c, 0] = term(c, (z - way_of(c) + Z) % Z).astype(BF)
        sum_copy(c, 0).start()

    def sum_step(s, carry):
        for c in (0, 2, 1, 3):
            j = (z - way_of(c) * (1 + s) + 2 * Z) % Z
            value = term(c, j)
            arrived(rrecv.at[c, s - 1], rs_recv.at[c, s - 1])
            rsend[c, s] = (value + rrecv[c, s - 1].astype(F32)).astype(BF)
            sum_copy(c, s).start()
        return carry

    lax.fori_loop(1, Z - 1, sum_step, 0)

    for c in (0, 2, 1, 3):
        value = term(c, z)
        arrived(rrecv.at[c, Z - 2], rs_recv.at[c, Z - 2])
        fin[c] = (value + rrecv[c, Z - 2].astype(F32)).astype(BF)

        def home(i, carry, c=c):
            to_e = (e + i) % EXPERTS
            to = to_e * Q + c
            src = fin.at[c, pl.ds(pl.multiple_of(to_e * TOK, TOK), TOK)]

            @pl.when(to != p)
            def _():
                remote(src, ret.at[p], a_send.at[0], a_recv.at[0], to, z).start()

            @pl.when(to == p)
            def _():
                pltpu.make_async_copy(src, ret.at[p], a_recv.at[0]).start()

            return carry

        lax.fori_loop(0, EXPERTS, home, 0)

    arrived(ret, a_recv.at[0])
    named, share = routes[...], rw[...]
    totals = [jnp.zeros((TOK, PIECE), F32) for _ in range(Q)]
    for x in range(EXPERTS):
        factor = jnp.sum(jnp.where(named == x, share, 0.0), axis=1, keepdims=True)
        for c in range(Q):
            totals[c] += factor * ret[x * Q + c].astype(F32)
    for c in range(Q):
        out[c] = totals[c].astype(BF)

    for copy in open_sends:
        copy.wait_send()

    @pl.when(shares)
    def _():
        for copy in g_copies:
            copy.wait_send()

    for c in range(Q):
        for s in range(Z - 1):
            sum_copy(c, s).wait_send()
    arrived(ret.at[pl.ds(0, EXPERTS * Q - 1)], a_send.at[0])


def local(tokens, routes, route_weights, gate_weight, up_weight, down_weight):
    dma = pltpu.SemaphoreType.DMA
    vmem = pl.BlockSpec(memory_space=pltpu.VMEM)
    anywhere = pl.BlockSpec(memory_space=pl.ANY)
    got = pl.pallas_call(
        kernel,
        out_shape=jax.ShapeDtypeStruct((Q, TOK, PIECE), BF),
        in_specs=[vmem, vmem, vmem, anywhere, anywhere, anywhere],
        out_specs=vmem,
        scratch_shapes=[
            pltpu.VMEM((Z, ROWS, HALF), BF),
            pltpu.VMEM((W, UNITS), BF),
            pltpu.VMEM((W, UNITS), BF),
            pltpu.VMEM((UNITS, W), BF),
            pltpu.VMEM((Z, UNITS, PIECE), BF),
            pltpu.VMEM((Q, ROWS, 2 * UNITS), F32),
            pltpu.VMEM((Q, ROWS, 2 * UNITS), BF),
            pltpu.VMEM((Q, Q - 1, SHARE, 2 * UNITS), BF),
            pltpu.VMEM((Q, ROWS, UNITS), BF),
            pltpu.VMEM((Q, Z - 1, ROWS, PIECE), BF),
            pltpu.VMEM((Q, Z - 1, ROWS, PIECE), BF),
            pltpu.VMEM((Q, ROWS, PIECE), BF),
            pltpu.VMEM((EXPERTS * Q, TOK, PIECE), BF),
            dma((3,)), dma((3,)), dma((1,)), dma((3,)), dma((3,)), dma((3,)), dma((3,)),
            dma((7,)), dma((7,)), dma((7,)), dma((7,)),
            dma((4, 3)), dma((4, 3)), dma((4, 3)), dma((4, 3)),
            dma((4, 7)), dma((4, 7)), dma((1,)), dma((1,)),
        ],
        compiler_params=pltpu.CompilerParams(
            collective_id=0, has_side_effects=True, vmem_limit_bytes=48 * 1024 * 1024
        ),
        cost_estimate=pl.CostEstimate(flops=3 * 10**9, bytes_accessed=4 * 10**6, transcendentals=10**5),
    )(tokens, routes, route_weights, gate_weight[0], up_weight[0], down_weight[0])
    return got.transpose(1, 0, 2).reshape(TOK, Q * PIECE)


def solution(mesh):
    placed = (
        P("expert", None),
        P("expert", None),
        P("expert", None),
        P("expert", None, "hsplit"),
        P("expert", None, "hsplit"),
        P("expert", "hsplit", None),
    )
    return jax.shard_map(
        local, mesh=mesh, in_specs=placed, out_specs=P("expert", "hsplit"), check_vma=False
    )
```

```python
import jax
import jax.numpy as jnp
from jax import lax
from jax.experimental import pallas as pl
from jax.experimental.pallas import tpu as pltpu
from jax.sharding import PartitionSpec as P

EXPERTS = 16
Q = 4
Z = 8
TOP = 8
LX = 4
LY = 4
TOK = 16
D = 7168
W = D // Q
PART = 384
REST = W - 2 * PART
PIECE = W // Z
UNITS = 256
ROWS = EXPERTS * TOK
SUB = ROWS // 2
SHARE = ROWS // Q
BF = jnp.bfloat16
F32 = jnp.float32


def kernel(
    tok_in, routes_in, rw_in, gate_in, up_in, down_in, out,
    tok, routes, rw, xb, bb, wg, wu, wd, dj, acc, pbuf, pcore, ybuf, py, hid, rsend, rrecv, fin, ret,
    w_sem, g_send, g_recv, b_send, b_recv, x_send, x_recv, y_send, y_recv, bx_send, bx_recv,
    up_send, up_recv, dn_send, dn_recv,
    p_send, p_recv, m_send, m_recv, h_send, h_recv, rs_send, rs_recv, a_send, a_recv,
):
    p = lax.axis_index("expert")
    z = lax.axis_index("hsplit")
    e, q = p // Q, p % Q
    ex, ey = e // LY, e % LY
    z_up, z_dn = (z + 1) % Z, (z + Z - 1) % Z
    open_sends = []

    def remote(src, dst, send, recv, to_p, to_z):
        return pltpu.make_async_remote_copy(
            src_ref=src, dst_ref=dst, send_sem=send, recv_sem=recv,
            device_id=(to_p, to_z), device_id_type=pl.DeviceIdType.MESH,
        )

    def send(*args):
        copy = remote(*args)
        copy.start()
        open_sends.append(copy)

    def arrived(ref, sem):
        pltpu.make_async_copy(ref, ref, sem).wait()

    def owner(x, y, k):
        return (x * LY + y) * Q + k

    def rows(start, count):
        return pl.ds(pl.multiple_of(start, 16), count)

    pairs = ((tok_in, tok), (gate_in, wg), (up_in, wu), (down_in, wd), (routes_in, routes), (rw_in, rw))
    loads = [pltpu.make_async_copy(src, dst, w_sem.at[i]) for i, (src, dst) in enumerate(pairs)]
    for load in loads:
        load.start()

    barrier = pltpu.get_barrier_semaphore()

    def greet(i, carry):
        pl.semaphore_signal(
            barrier, inc=1, device_id=((p + i) % (EXPERTS * Q), z), device_id_type=pl.DeviceIdType.MESH
        )
        return carry

    lax.fori_loop(1, EXPERTS * Q, greet, 0)
    for to_z in (z_up, z_dn):
        pl.semaphore_signal(barrier, inc=1, device_id=(p, to_z), device_id_type=pl.DeviceIdType.MESH)
    loads[0].wait()
    pl.semaphore_wait(barrier, EXPERTS * Q + 1)

    side = jnp.where(z % 2 == 1, 1, Q - 1)
    own_group = z // 2
    order = (own_group, (own_group + side) % Q, (own_group + 2 * Q - side) % Q, (own_group + 2) % Q)
    column = LY * TOK
    own_rows = rows(e * TOK, TOK)

    mine = xb.at[z, own_rows]
    shares = q == z // 2

    def share_of(to_q):
        return tok.at[:, pl.ds(pl.multiple_of(to_q * W + (z % 2) * PART, 128), PART)]

    g_copies = [
        remote(
            share_of((q + d % Q) % Q), mine, g_send.at[d], g_recv.at[0],
            owner(ex, (ey + d // Q) % LY, (q + d % Q) % Q), z,
        )
        for d in range(1, Q * LY)
    ]
    own_share = pltpu.make_async_copy(share_of(q), mine, g_recv.at[0])

    def rest_of(to_q):
        return tok.at[:, pl.ds(pl.multiple_of(to_q * W + 2 * PART, 128), REST)]

    own_rest = pltpu.make_async_copy(rest_of(q), bb.at[q, own_rows], b_recv.at[0])
    for d in range(1, Q):
        to = (q + d) % Q
        send(rest_of(to), bb.at[q, own_rows], b_send.at[d], b_recv.at[d], e * Q + to, z)
    own_rest.start()

    @pl.when(shares)
    def _():
        for copy in g_copies:
            copy.start()
        own_share.start()

    own_rest.wait()
    for d in range(1, Q):
        arrived(bb.at[(q + Q - d) % Q, own_rows], b_recv.at[d])

    def y_sends(i):
        ref = bb.at[order[i], own_rows]
        for d in (1, 3, 2):
            send(ref, ref, y_send.at[i, d], y_recv.at[i, d], owner(ex, (ey + d) % LY, q), z)

    def y_arrived(i):
        for d in (1, 3, 2):
            arrived(bb.at[order[i], rows((ex * LY + (ey + LY - d) % LY) * TOK, TOK)], y_recv.at[i, d])

    x_up, x_dn = (ex + 1) % LX, (ex + LX - 1) % LX
    x_far = (ex + 2) % LX

    def x_sends(i):
        ref = bb.at[order[i], rows(ex * column, column)]
        send(ref, ref, bx_send.at[i, 0], bx_recv.at[i, 0], owner(x_up, ey, q), z)
        send(ref, ref, bx_send.at[i, 1], bx_recv.at[i, 1], owner(x_dn, ey, q), z)

    def x_forward(i):
        half = column // 2
        arrived(bb.at[order[i], rows(x_dn * column, column)], bx_recv.at[i, 0])
        ref = bb.at[order[i], rows(x_dn * column, half)]
        send(ref, ref, bx_send.at[i, 2], bx_recv.at[i, 2], owner(x_up, ey, q), z)
        arrived(bb.at[order[i], rows(x_up * column, column)], bx_recv.at[i, 1])
        ref = bb.at[order[i], rows(x_up * column + half, half)]
        send(ref, ref, bx_send.at[i, 3], bx_recv.at[i, 3], owner(x_dn, ey, q), z)

    def x_arrived(i):
        half = column // 2
        arrived(bb.at[order[i], rows(x_far * column, half)], bx_recv.at[i, 2])
        arrived(bb.at[order[i], rows(x_far * column + half, half)], bx_recv.at[i, 3])

    y_sends(0)
    mine_x = xb.at[z, rows(ex * column, column)]
    arrived(mine_x, g_recv.at[0])
    for d in range(1, LX):
        send(mine_x, mine_x, x_send.at[d], x_recv.at[d], owner((ex + d) % LX, ey, q), z)
    for i in range(1, Q):
        y_sends(i)
    for load in loads[1:]:
        load.wait()
    y_arrived(0)
    x_sends(0)
    for d in range(1, LX):
        arrived(xb.at[z, rows(((ex + LX - d) % LX) * column, column)], x_recv.at[d])

    steps = 7

    def half_of(block, k, way):
        which = k % 2 if way > 0 else (k + 1) % 2
        return xb.at[block, pl.ds(which * SUB, SUB)]

    def ring_send(k, way):
        block = (z - way * (k // 2) + Z) % Z
        ref = half_of(block, k, way)
        if way > 0:
            send(ref, ref, up_send.at[k], up_recv.at[k], p, z_up)
        else:
            send(ref, ref, dn_send.at[k], dn_recv.at[k], p, z_dn)

    def ring_step(k):
        for way in (1, -1):
            block = (z - way * (k // 2 + 1) + 2 * Z) % Z
            arrived(half_of(block, k, way), (up_recv if way > 0 else dn_recv).at[k])
            if k + 2 < steps:
                ring_send(k + 2, way)

    def add_terms(group, x, wrows, first):
        for at, w in ((0, wg), (UNITS, wu)):
            value = jnp.dot(x, w[wrows, :], preferred_element_type=F32)
            if first:
                acc[group, :, at : at + UNITS] = value
            else:
                acc[group, :, at : at + UNITS] += value

    def add_block(block, first):
        add_terms(block // 2, xb[block], pl.ds(pl.multiple_of((block % 2) * PART, 128), PART), first)

    def add_rest(i):
        x_arrived(i)
        add_terms(order[i], bb[order[i]], pl.ds(2 * PART, REST), False)

    core, chip = q % 2, q // 2

    def share_row(k):
        return (k % 2) * 2 * SHARE + (k // 2) * SHARE

    def share_partials(i):
        pbuf[i] = acc[order[i], rows((1 - core) * 2 * SHARE, 2 * SHARE), :].astype(BF)
        send(pbuf.at[i], pcore.at[i], p_send.at[i], p_recv.at[i], e * Q + chip * 2 + 1 - core, z)

    def cross(i):
        far, near = rows((1 - chip) * SHARE, SHARE), rows(chip * SHARE, SHARE)
        far_row = core * 2 * SHARE + (1 - chip) * SHARE
        arrived(pcore.at[i], p_recv.at[i])
        ybuf[i] = (acc[order[i], rows(far_row, SHARE), :] + pcore[i, far, :].astype(F32)).astype(BF)
        send(ybuf.at[i], py.at[i], m_send.at[i], m_recv.at[i], e * Q + (1 - chip) * 2 + core, z)
        acc[order[i], rows(share_row(q), SHARE), :] += pcore[i, near, :].astype(F32)

    def share_hidden(i):
        here = rows(share_row(q), SHARE)
        arrived(py.at[i], m_recv.at[i])
        total = acc[order[i], here, :] + py[i].astype(F32)
        g, u = total[:, :UNITS], total[:, UNITS:]
        hid[order[i], here, :] = (g / (1.0 + jnp.exp(-g)) * u).astype(BF)
        ref = hid.at[order[i], here]
        for d in range(1, Q):
            send(ref, ref, h_send.at[i, d], h_recv.at[i, d], e * Q + (q + d) % Q, z)

    even = z % 2 == 0

    def nth(up, down):
        return jnp.where(even, (z + up) % Z, (z + down) % Z)

    for k in (0, 1):
        ring_send(k, 1)
        ring_send(k, -1)
    add_block(z, True)
    for j in range(Z):
        dj[j] = wd[:, j * PIECE : (j + 1) * PIECE]
    y_arrived(1)
    x_sends(1)
    ring_step(0)
    x_forward(0)
    ring_step(1)
    add_block(nth(1, Z - 1), False)
    add_rest(0)
    share_partials(0)
    y_arrived(2)
    x_sends(2)
    ring_step(2)
    x_forward(1)
    add_block(nth(Z - 1, 1), True)
    cross(0)
    ring_step(3)
    add_block(nth(Z - 2, 2), False)
    add_rest(1)
    share_partials(1)
    share_hidden(0)
    y_arrived(3)
    x_sends(3)
    ring_step(4)
    x_forward(2)
    add_block(nth(2, Z - 2), True)
    cross(1)
    ring_step(5)
    add_block(nth(3, Z - 3), False)
    add_rest(2)
    share_partials(2)
    share_hidden(1)
    x_forward(3)
    add_block(nth(Z - 3, 3), True)
    cross(2)
    ring_step(6)
    add_block((z + 4) % Z, False)
    share_hidden(2)
    add_rest(3)
    share_partials(3)
    cross(3)
    share_hidden(3)
    for i in range(Q):
        for d in range(1, Q):
            arrived(hid.at[order[i], rows(share_row((q + Q - d) % Q), SHARE)], h_recv.at[i, d])

    def way_of(c):
        return 1 if c < 2 else -1

    def sum_copy(c, s):
        return remote(
            rsend.at[c, s], rrecv.at[c, s], rs_send.at[c, s], rs_recv.at[c, s],
            p, z_up if way_of(c) > 0 else z_dn,
        )

    def term(c, j):
        return jnp.dot(hid[c], dj[j], preferred_element_type=F32)

    for c in (0, 2, 1, 3):
        rsend[c, 0] = term(c, (z - way_of(c) + Z) % Z).astype(BF)
        sum_copy(c, 0).start()

    def sum_step(s, carry):
        for c in (0, 2, 1, 3):
            j = (z - way_of(c) * (1 + s) + 2 * Z) % Z
            value = term(c, j)
            arrived(rrecv.at[c, s - 1], rs_recv.at[c, s - 1])
            rsend[c, s] = (value + rrecv[c, s - 1].astype(F32)).astype(BF)
            sum_copy(c, s).start()
        return carry

    lax.fori_loop(1, Z - 1, sum_step, 0)

    for c in (0, 2, 1, 3):
        value = term(c, z)
        arrived(rrecv.at[c, Z - 2], rs_recv.at[c, Z - 2])
        fin[c] = (value + rrecv[c, Z - 2].astype(F32)).astype(BF)

        def home(i, carry, c=c):
            to_e = (e + i) % EXPERTS
            to = to_e * Q + c
            src = fin.at[c, pl.ds(pl.multiple_of(to_e * TOK, TOK), TOK)]

            @pl.when(to != p)
            def _():
                remote(src, ret.at[p], a_send.at[0], a_recv.at[0], to, z).start()

            @pl.when(to == p)
            def _():
                pltpu.make_async_copy(src, ret.at[p], a_recv.at[0]).start()

            return carry

        lax.fori_loop(0, EXPERTS, home, 0)

    arrived(ret, a_recv.at[0])
    named, share = routes[...], rw[...]
    lane = lax.broadcasted_iota(jnp.int32, (TOK, TOK), 1)
    diagonal = lane == lax.broadcasted_iota(jnp.int32, (TOK, TOK), 0)
    totals = [jnp.zeros((TOK, PIECE), F32) for _ in range(Q)]
    for x in range(EXPERTS):
        row = jnp.sum(jnp.where(named == x, share, 0.0), axis=0, keepdims=True)
        factor = jnp.sum(jnp.where(diagonal, row, 0.0), axis=1, keepdims=True)
        for c in range(Q):
            totals[c] += factor * ret[x * Q + c].astype(F32)
    for c in range(Q):
        out[c] = totals[c].astype(BF)

    for copy in open_sends:
        copy.wait_send()

    @pl.when(shares)
    def _():
        for copy in g_copies:
            copy.wait_send()

    for c in range(Q):
        for s in range(Z - 1):
            sum_copy(c, s).wait_send()
    arrived(ret.at[pl.ds(0, EXPERTS * Q - 1)], a_send.at[0])


def local(tokens, routes, route_weights, gate_weight, up_weight, down_weight):
    dma = pltpu.SemaphoreType.DMA
    vmem = pl.BlockSpec(memory_space=pltpu.VMEM)
    anywhere = pl.BlockSpec(memory_space=pl.ANY)
    got = pl.pallas_call(
        kernel,
        out_shape=jax.ShapeDtypeStruct((Q, TOK, PIECE), BF),
        in_specs=[anywhere] * 6,
        out_specs=vmem,
        scratch_shapes=[
            pltpu.VMEM((TOK, D), BF),
            pltpu.VMEM((TOP, TOK), jnp.int32),
            pltpu.VMEM((TOP, TOK), F32),
            pltpu.VMEM((Z, ROWS, PART), BF),
            pltpu.VMEM((Q, ROWS, REST), BF),
            pltpu.VMEM((W, UNITS), BF),
            pltpu.VMEM((W, UNITS), BF),
            pltpu.VMEM((UNITS, W), BF),
            pltpu.VMEM((Z, UNITS, PIECE), BF),
            pltpu.VMEM((Q, ROWS, 2 * UNITS), F32),
            pltpu.VMEM((Q, 2 * SHARE, 2 * UNITS), BF),
            pltpu.VMEM((Q, 2 * SHARE, 2 * UNITS), BF),
            pltpu.VMEM((Q, SHARE, 2 * UNITS), BF),
            pltpu.VMEM((Q, SHARE, 2 * UNITS), BF),
            pltpu.VMEM((Q, ROWS, UNITS), BF),
            pltpu.VMEM((Q, Z - 1, ROWS, PIECE), BF),
            pltpu.VMEM((Q, Z - 1, ROWS, PIECE), BF),
            pltpu.VMEM((Q, ROWS, PIECE), BF),
            pltpu.VMEM((EXPERTS * Q, TOK, PIECE), BF),
            dma((6,)), dma((16,)), dma((1,)), dma((4,)), dma((4,)), dma((4,)), dma((4,)),
            dma((4, 4)), dma((4, 4)), dma((4, 4)), dma((4, 4)),
            dma((7,)), dma((7,)), dma((7,)), dma((7,)),
            dma((4,)), dma((4,)), dma((4,)), dma((4,)), dma((4, 4)), dma((4, 4)),
            dma((4, 7)), dma((4, 7)), dma((1,)), dma((1,)),
        ],
        compiler_params=pltpu.CompilerParams(
            collective_id=0, has_side_effects=True, vmem_limit_bytes=60 * 1024 * 1024
        ),
        cost_estimate=pl.CostEstimate(flops=3 * 10**9, bytes_accessed=4 * 10**6, transcendentals=10**5),
    )(tokens, routes.T, route_weights.T, gate_weight[0], up_weight[0], down_weight[0])
    return got.transpose(1, 0, 2).reshape(TOK, Q * PIECE)


def solution(mesh):
    placed = (
        P("expert", None),
        P("expert", None),
        P("expert", None),
        P("expert", None, "hsplit"),
        P("expert", None, "hsplit"),
        P("expert", "hsplit", None),
    )
    return jax.shard_map(
        local, mesh=mesh, in_specs=placed, out_specs=P("expert", "hsplit"), check_vma=False
    )
```

```python
import jax
import jax.numpy as jnp
from jax import lax
from jax.experimental import pallas as pl
from jax.experimental.pallas import tpu as pltpu
from jax.sharding import PartitionSpec as P

EXPERTS = 16
Q = 4
Z = 8
TOP = 8
LX = 4
LY = 4
TOK = 16
D = 7168
W = D // Q
PART = 384
REST = W - 2 * PART
PIECE = W // Z
UNITS = 256
ROWS = EXPERTS * TOK
SUB = ROWS // 2
SHARE = ROWS // Q
BF = jnp.bfloat16
F32 = jnp.float32


def kernel(
    tok_in, routes_in, rw_in, gate_in, up_in, down_in, out,
    tok, routes, rw, xb, bb, wg, wu, wd, dj, acc, pbuf, pcore, ybuf, py, hid,
    fmat, wbuf, rsend, rrecv, fin, ret, tx1, rx1, tx2, rx2, ty, ry, tz, rz,
    w_sem, g_send, g_recv, b_send, b_recv, x_send, x_recv, y_send, y_recv, bx_send, bx_recv,
    up_send, up_recv, dn_send, dn_recv,
    p_send, p_recv, m_send, m_recv, h_send, h_recv, rs_send, rs_recv, a_send, a_recv,
    f_send, f_recv, r1_send, r1_recv, r2_send, r2_recv, ry_send, ry_recv, rz_send, rz_recv,
):
    p = lax.axis_index("expert")
    z = lax.axis_index("hsplit")
    e, q = p // Q, p % Q
    ex, ey = e // LY, e % LY
    z_up, z_dn = (z + 1) % Z, (z + Z - 1) % Z
    open_sends = []

    def remote(src, dst, send, recv, to_p, to_z):
        return pltpu.make_async_remote_copy(
            src_ref=src, dst_ref=dst, send_sem=send, recv_sem=recv,
            device_id=(to_p, to_z), device_id_type=pl.DeviceIdType.MESH,
        )

    def send(*args):
        copy = remote(*args)
        copy.start()
        open_sends.append(copy)

    def arrived(ref, sem):
        pltpu.make_async_copy(ref, ref, sem).wait()

    def owner(x, y, k):
        return (x * LY + y) * Q + k

    def rows(start, count):
        return pl.ds(pl.multiple_of(start, 16), count)

    pairs = ((tok_in, tok), (routes_in, routes), (rw_in, rw), (gate_in, wg), (up_in, wu), (down_in, wd))
    loads = [pltpu.make_async_copy(src, dst, w_sem.at[i]) for i, (src, dst) in enumerate(pairs)]
    for load in loads:
        load.start()

    barrier = pltpu.get_barrier_semaphore()

    def greet(i, carry):
        pl.semaphore_signal(
            barrier, inc=1, device_id=((p + i) % (EXPERTS * Q), z), device_id_type=pl.DeviceIdType.MESH
        )
        return carry

    lax.fori_loop(1, EXPERTS * Q, greet, 0)

    def greet_z(i, carry):
        pl.semaphore_signal(
            barrier, inc=1, device_id=(e * Q + i % Q, (z + i // Q) % Z), device_id_type=pl.DeviceIdType.MESH
        )
        return carry

    lax.fori_loop(Q, Z * Q, greet_z, 0)
    for load in loads[:3]:
        load.wait()

    named, share = routes[...], rw[...]
    lane = lax.broadcasted_iota(jnp.int32, (TOK, TOK), 1)
    diagonal = lane == lax.broadcasted_iota(jnp.int32, (TOK, TOK), 0)
    wide = lax.broadcasted_iota(jnp.int32, (TOK, 128), 1)
    factors = jnp.zeros((TOK, 128), F32)
    for x in range(EXPERTS):
        row = jnp.sum(jnp.where(named == x, share, 0.0), axis=0, keepdims=True)
        factor = jnp.sum(jnp.where(diagonal, row, 0.0), axis=1, keepdims=True)
        factors = jnp.where(wide == x, factor, factors)
    fmat[...] = factors
    pl.semaphore_wait(barrier, EXPERTS * Q - 1 + (Z - 1) * Q)

    side = jnp.where(z % 2 == 1, 1, Q - 1)
    own_group = z // 2
    order = (own_group, (own_group + side) % Q, (own_group + 2 * Q - side) % Q, (own_group + 2) % Q)
    column = LY * TOK
    own_rows = rows(e * TOK, TOK)

    mine = xb.at[z, own_rows]
    shares = q == z // 2

    def share_of(to_q):
        return tok.at[:, pl.ds(pl.multiple_of(to_q * W + (z % 2) * PART, 128), PART)]

    g_copies = [
        remote(
            share_of((q + d % Q) % Q), mine, g_send.at[d], g_recv.at[0],
            owner(ex, (ey + d // Q) % LY, (q + d % Q) % Q), z,
        )
        for d in range(1, Q * LY)
    ]
    own_share = pltpu.make_async_copy(share_of(q), mine, g_recv.at[0])

    def rest_of(to_q):
        return tok.at[:, pl.ds(pl.multiple_of(to_q * W + 2 * PART, 128), REST)]

    own_rest = pltpu.make_async_copy(rest_of(q), bb.at[q, own_rows], b_recv.at[0])
    for d in range(1, Q):
        to = (q + d) % Q
        send(rest_of(to), bb.at[q, own_rows], b_send.at[d], b_recv.at[d], e * Q + to, z)
    own_rest.start()

    @pl.when(shares)
    def _():
        for copy in g_copies:
            copy.start()
        own_share.start()

    own_rest.wait()
    for d in range(1, Q):
        arrived(bb.at[(q + Q - d) % Q, own_rows], b_recv.at[d])

    def y_sends(i):
        ref = bb.at[order[i], own_rows]
        for d in (1, 3, 2):
            send(ref, ref, y_send.at[i, d], y_recv.at[i, d], owner(ex, (ey + d) % LY, q), z)

    def y_arrived(i):
        for d in (1, 3, 2):
            arrived(bb.at[order[i], rows((ex * LY + (ey + LY - d) % LY) * TOK, TOK)], y_recv.at[i, d])

    x_up, x_dn = (ex + 1) % LX, (ex + LX - 1) % LX
    x_far = (ex + 2) % LX

    def x_sends(i):
        ref = bb.at[order[i], rows(ex * column, column)]
        send(ref, ref, bx_send.at[i, 0], bx_recv.at[i, 0], owner(x_up, ey, q), z)
        send(ref, ref, bx_send.at[i, 1], bx_recv.at[i, 1], owner(x_dn, ey, q), z)

    def x_forward(i):
        half = column // 2
        arrived(bb.at[order[i], rows(x_dn * column, column)], bx_recv.at[i, 0])
        ref = bb.at[order[i], rows(x_dn * column, half)]
        send(ref, ref, bx_send.at[i, 2], bx_recv.at[i, 2], owner(x_up, ey, q), z)
        arrived(bb.at[order[i], rows(x_up * column, column)], bx_recv.at[i, 1])
        ref = bb.at[order[i], rows(x_up * column + half, half)]
        send(ref, ref, bx_send.at[i, 3], bx_recv.at[i, 3], owner(x_dn, ey, q), z)

    def x_arrived(i):
        half = column // 2
        arrived(bb.at[order[i], rows(x_far * column, half)], bx_recv.at[i, 2])
        arrived(bb.at[order[i], rows(x_far * column + half, half)], bx_recv.at[i, 3])

    y_sends(0)
    mine_x = xb.at[z, rows(ex * column, column)]
    arrived(mine_x, g_recv.at[0])
    for d in range(1, LX):
        send(mine_x, mine_x, x_send.at[d], x_recv.at[d], owner((ex + d) % LX, ey, q), z)
    for i in range(1, Q):
        y_sends(i)

    def share_factors(i, carry):
        to = (e + i) % EXPERTS * Q + share_of_column

        @pl.when(to != p)
        def _():
            remote(fmat, wbuf.at[q, ey], f_send.at[i], f_recv.at[0], to, z).start()

        @pl.when(to == p)
        def _():
            pltpu.make_async_copy(fmat, wbuf.at[q, ey], f_recv.at[0]).start()

        return carry

    share_of_column = (ex % 2) * 2 + ex // 2
    lax.fori_loop(0, EXPERTS, share_factors, 0)
    for load in loads[3:]:
        load.wait()
    y_arrived(0)
    x_sends(0)
    for d in range(1, LX):
        arrived(xb.at[z, rows(((ex + LX - d) % LX) * column, column)], x_recv.at[d])

    steps = 7

    def half_of(block, k, way):
        which = k % 2 if way > 0 else (k + 1) % 2
        return xb.at[block, pl.ds(which * SUB, SUB)]

    def ring_send(k, way):
        block = (z - way * (k // 2) + Z) % Z
        ref = half_of(block, k, way)
        if way > 0:
            send(ref, ref, up_send.at[k], up_recv.at[k], p, z_up)
        else:
            send(ref, ref, dn_send.at[k], dn_recv.at[k], p, z_dn)

    def ring_step(k):
        for way in (1, -1):
            block = (z - way * (k // 2 + 1) + 2 * Z) % Z
            arrived(half_of(block, k, way), (up_recv if way > 0 else dn_recv).at[k])
            if k + 2 < steps:
                ring_send(k + 2, way)

    def add_terms(group, x, wrows, first):
        for at, w in ((0, wg), (UNITS, wu)):
            value = jnp.dot(x, w[wrows, :], preferred_element_type=F32)
            if first:
                acc[group, :, at : at + UNITS] = value
            else:
                acc[group, :, at : at + UNITS] += value

    def add_block(block, first):
        add_terms(block // 2, xb[block], pl.ds(pl.multiple_of((block % 2) * PART, 128), PART), first)

    def add_rest(i):
        x_arrived(i)
        add_terms(order[i], bb[order[i]], pl.ds(2 * PART, REST), False)

    core, chip = q % 2, q // 2

    def share_row(k):
        return (k % 2) * 2 * SHARE + (k // 2) * SHARE

    def share_partials(i):
        pbuf[i] = acc[order[i], rows((1 - core) * 2 * SHARE, 2 * SHARE), :].astype(BF)
        send(pbuf.at[i], pcore.at[i], p_send.at[i], p_recv.at[i], e * Q + chip * 2 + 1 - core, z)

    def cross(i):
        far, near = rows((1 - chip) * SHARE, SHARE), rows(chip * SHARE, SHARE)
        far_row = core * 2 * SHARE + (1 - chip) * SHARE
        arrived(pcore.at[i], p_recv.at[i])
        ybuf[i] = (acc[order[i], rows(far_row, SHARE), :] + pcore[i, far, :].astype(F32)).astype(BF)
        send(ybuf.at[i], py.at[i], m_send.at[i], m_recv.at[i], e * Q + (1 - chip) * 2 + core, z)
        acc[order[i], rows(share_row(q), SHARE), :] += pcore[i, near, :].astype(F32)

    def share_hidden(i):
        here = rows(share_row(q), SHARE)
        arrived(py.at[i], m_recv.at[i])
        total = acc[order[i], here, :] + py[i].astype(F32)
        g, u = total[:, :UNITS], total[:, UNITS:]
        if i == 0:
            arrived(wbuf, f_recv.at[0])
        factor = wbuf[order[i]].reshape(SHARE, 128)
        at_expert = lax.broadcasted_iota(jnp.int32, (SHARE, 128), 1) == e
        factor = jnp.sum(jnp.where(at_expert, factor, 0.0), axis=1, keepdims=True)
        hid[order[i], here, :] = (g / (1.0 + jnp.exp(-g)) * u * factor).astype(BF)
        ref = hid.at[order[i], here]
        for d in range(1, Q):
            send(ref, ref, h_send.at[i, d], h_recv.at[i, d], e * Q + (q + d) % Q, z)

    even = z % 2 == 0

    def nth(up, down):
        return jnp.where(even, (z + up) % Z, (z + down) % Z)

    for k in (0, 1):
        ring_send(k, 1)
        ring_send(k, -1)
    add_block(z, True)
    for j in range(Z):
        dj[j] = wd[:, j * PIECE : (j + 1) * PIECE]
    y_arrived(1)
    x_sends(1)
    ring_step(0)
    x_forward(0)
    ring_step(1)
    add_block(nth(1, Z - 1), False)
    add_rest(0)
    share_partials(0)
    y_arrived(2)
    x_sends(2)
    ring_step(2)
    x_forward(1)
    add_block(nth(Z - 1, 1), True)
    cross(0)
    ring_step(3)
    add_block(nth(Z - 2, 2), False)
    add_rest(1)
    share_partials(1)
    share_hidden(0)
    y_arrived(3)
    x_sends(3)
    ring_step(4)
    x_forward(2)
    add_block(nth(2, Z - 2), True)
    cross(1)
    ring_step(5)
    add_block(nth(3, Z - 3), False)
    add_rest(2)
    share_partials(2)
    share_hidden(1)
    x_forward(3)
    add_block(nth(Z - 3, 3), True)
    cross(2)
    ring_step(6)
    add_block((z + 4) % Z, False)
    share_hidden(2)
    add_rest(3)
    share_partials(3)
    cross(3)
    share_hidden(3)
    for i in range(Q):
        for d in range(1, Q):
            arrived(hid.at[order[i], rows(share_row((q + Q - d) % Q), SHARE)], h_recv.at[i, d])

    chunks = (0, 2, 1, 3)

    def way_of(c):
        return 1 if c < 2 else -1

    def sum_copy(c, s):
        return remote(
            rsend.at[c, s], rrecv.at[c, s], rs_send.at[c, s], rs_recv.at[c, s],
            p, z_up if way_of(c) > 0 else z_dn,
        )

    def term(c, j):
        return jnp.dot(hid[c // 2, c % 2 * SUB : (c % 2 + 1) * SUB, :], dj[j], preferred_element_type=F32)

    def sum_step(s):
        for c in chunks:
            j = (z - way_of(c) * (1 + s) + 2 * Z) % Z
            value = term(c, j)
            if s > 0:
                arrived(rrecv.at[c, s - 1], rs_recv.at[c, s - 1])
                value += rrecv[c, s - 1].astype(F32)
            rsend[c, s] = value.astype(BF)
            sum_copy(c, s).start()

    def sum_last(c):
        value = term(c, z)
        arrived(rrecv.at[c, Z - 2], rs_recv.at[c, Z - 2])
        fin[c] = (value + rrecv[c, Z - 2].astype(F32)).astype(BF)

        def home(i, carry):
            to_e = c % 2 * (EXPERTS // 2) + (e + i) % (EXPERTS // 2)
            to = to_e * Q + c // 2
            src = fin.at[c, rows((e + i) % (EXPERTS // 2) * TOK, TOK)]

            @pl.when(to != p)
            def _():
                remote(src, ret.at[p], a_send.at[0], a_recv.at[0], to, z).start()

            @pl.when(to == p)
            def _():
                pltpu.make_async_copy(src, ret.at[p], a_recv.at[0]).start()

            return carry

        lax.fori_loop(0, EXPERTS // 2, home, 0)

    half = column // 2

    def full_term(t, x):
        return jnp.dot(hid[2 + t, rows(x * column, column), :], wd[...], preferred_element_type=F32)

    def plane_far(t):
        tx1[t] = full_term(t, x_far).astype(BF)
        send(tx1.at[t, :half], rx1.at[t, 0], r1_send.at[t, 0], r1_recv.at[t, 0], owner(x_up, ey, q), z)
        send(tx1.at[t, half:], rx1.at[t, 1], r1_send.at[t, 1], r1_recv.at[t, 1], owner(x_dn, ey, q), z)

    def plane_near(t):
        for w, x in ((0, x_up), (1, x_dn)):
            value = full_term(t, x)
            mid, rest = slice(w * half, w * half + half), slice((1 - w) * half, (1 - w) * half + half)
            tx2[t, w, rest, :] = value[rest].astype(BF)
            arrived(rx1.at[t, w], r1_recv.at[t, w])
            tx2[t, w, mid, :] = (value[mid] + rx1[t, w].astype(F32)).astype(BF)
            send(tx2.at[t, w], rx2.at[t, w], r2_send.at[t, w], r2_recv.at[t, w], owner(x, ey, q), z)

    def plane_y(t):
        value = full_term(t, ex)
        for w in (0, 1):
            arrived(rx2.at[t, w], r2_recv.at[t, w])
            value += rx2[t, w].astype(F32)
        ty[t] = value.astype(BF)
        for d in (1, 3, 2):
            to = (ey + d) % LY
            send(
                ty.at[t, rows(to * TOK, TOK)], ry.at[t, d - 1], ry_send.at[t, d - 1], ry_recv.at[t, d - 1],
                owner(ex, to, q), z,
            )

    def home_copy(t, j):
        return remote(tz.at[t, j], rz.at[q, z], rz_send.at[t, j], rz_recv.at[0], e * Q + 2 + t, j)

    def is_here(t, j):
        return jnp.logical_and(q == 2 + t, z == j)

    def plane_home(t):
        value = ty[t, rows(ey * TOK, TOK), :].astype(F32)
        for d in (1, 3, 2):
            arrived(ry.at[t, d - 1], ry_recv.at[t, d - 1])
            value += ry[t, d - 1].astype(F32)
        for j in range(Z):
            tz[t, j] = value[:, j * PIECE : (j + 1) * PIECE].astype(BF)
        for j in range(Z):

            @pl.when(jnp.logical_not(is_here(t, j)))
            def _(j=j):
                home_copy(t, j).start()

            @pl.when(is_here(t, j))
            def _(j=j):
                pltpu.make_async_copy(tz.at[t, j], rz.at[q, z], rz_recv.at[0]).start()

    sum_step(0)
    plane_far(0)
    plane_far(1)
    sum_step(1)
    plane_near(0)
    sum_step(2)
    plane_near(1)
    sum_step(3)
    sum_step(4)
    plane_y(0)
    sum_step(5)
    plane_y(1)
    sum_step(6)
    plane_home(0)
    for c in chunks:
        sum_last(c)
    plane_home(1)

    @pl.when(q < 2)
    def _():
        arrived(ret, a_recv.at[0])
        for k in range(Q):
            total = ret[k].astype(F32)
            for x in range(1, EXPERTS):
                total += ret[x * Q + k].astype(F32)
            out[k] = total.astype(BF)
        arrived(ret.at[pl.ds(0, 2 * EXPERTS - 1)], a_send.at[0])

    @pl.when(q >= 2)
    def _():
        arrived(rz, rz_recv.at[0])
        for k in range(Q):
            total = rz[k, 0].astype(F32)
            for j in range(1, Z):
                total += rz[k, j].astype(F32)
            out[k] = total.astype(BF)
        arrived(ret.at[pl.ds(0, 2 * EXPERTS)], a_send.at[0])

    for copy in open_sends:
        copy.wait_send()

    @pl.when(shares)
    def _():
        for copy in g_copies:
            copy.wait_send()

    def factors_sent(i, carry):
        to = (e + i) % EXPERTS * Q + share_of_column

        @pl.when(to != p)
        def _():
            remote(fmat, wbuf.at[q, ey], f_send.at[i], f_recv.at[0], to, z).wait_send()

        return carry

    lax.fori_loop(0, EXPERTS, factors_sent, 0)
    for c in range(Q):
        for s in range(Z - 1):
            sum_copy(c, s).wait_send()
    for t in range(2):
        for j in range(Z):

            @pl.when(jnp.logical_not(is_here(t, j)))
            def _(t=t, j=j):
                home_copy(t, j).wait_send()


def local(tokens, routes, route_weights, gate_weight, up_weight, down_weight):
    dma = pltpu.SemaphoreType.DMA
    vmem = pl.BlockSpec(memory_space=pltpu.VMEM)
    anywhere = pl.BlockSpec(memory_space=pl.ANY)
    got = pl.pallas_call(
        kernel,
        out_shape=jax.ShapeDtypeStruct((Q, TOK, PIECE), BF),
        in_specs=[anywhere] * 6,
        out_specs=vmem,
        scratch_shapes=[
            pltpu.VMEM((TOK, D), BF),
            pltpu.VMEM((TOP, TOK), jnp.int32),
            pltpu.VMEM((TOP, TOK), F32),
            pltpu.VMEM((Z, ROWS, PART), BF),
            pltpu.VMEM((Q, ROWS, REST), BF),
            pltpu.VMEM((W, UNITS), BF),
            pltpu.VMEM((W, UNITS), BF),
            pltpu.VMEM((UNITS, W), BF),
            pltpu.VMEM((Z, UNITS, PIECE), BF),
            pltpu.VMEM((Q, ROWS, 2 * UNITS), F32),
            pltpu.VMEM((Q, 2 * SHARE, 2 * UNITS), BF),
            pltpu.VMEM((Q, 2 * SHARE, 2 * UNITS), BF),
            pltpu.VMEM((Q, SHARE, 2 * UNITS), BF),
            pltpu.VMEM((Q, SHARE, 2 * UNITS), BF),
            pltpu.VMEM((Q, ROWS, UNITS), BF),
            pltpu.VMEM((TOK, 128), F32),
            pltpu.VMEM((Q, LY, TOK, 128), F32),
            pltpu.VMEM((Q, Z - 1, SUB, PIECE), BF),
            pltpu.VMEM((Q, Z - 1, SUB, PIECE), BF),
            pltpu.VMEM((Q, SUB, PIECE), BF),
            pltpu.VMEM((EXPERTS * Q, TOK, PIECE), BF),
            pltpu.VMEM((2, SHARE, W), BF),
            pltpu.VMEM((2, 2, SHARE // 2, W), BF),
            pltpu.VMEM((2, 2, SHARE, W), BF),
            pltpu.VMEM((2, 2, SHARE, W), BF),
            pltpu.VMEM((2, SHARE, W), BF),
            pltpu.VMEM((2, LY - 1, TOK, W), BF),
            pltpu.VMEM((2, Z, TOK, PIECE), BF),
            pltpu.VMEM((Q, Z, TOK, PIECE), BF),
            dma((6,)), dma((16,)), dma((1,)), dma((4,)), dma((4,)), dma((4,)), dma((4,)),
            dma((4, 4)), dma((4, 4)), dma((4, 4)), dma((4, 4)),
            dma((7,)), dma((7,)), dma((7,)), dma((7,)),
            dma((4,)), dma((4,)), dma((4,)), dma((4,)), dma((4, 4)), dma((4, 4)),
            dma((4, 7)), dma((4, 7)), dma((1,)), dma((1,)),
            dma((16,)), dma((1,)), dma((2, 2)), dma((2, 2)), dma((2, 2)), dma((2, 2)),
            dma((2, 3)), dma((2, 3)), dma((2, 8)), dma((1,)),
        ],
        compiler_params=pltpu.CompilerParams(
            collective_id=0, has_side_effects=True, vmem_limit_bytes=60 * 1024 * 1024
        ),
        cost_estimate=pl.CostEstimate(flops=3 * 10**9, bytes_accessed=4 * 10**6, transcendentals=10**5),
    )(tokens, routes.T, route_weights.T, gate_weight[0], up_weight[0], down_weight[0])
    return got.transpose(1, 0, 2).reshape(TOK, Q * PIECE)


def solution(mesh):
    placed = (
        P("expert", None),
        P("expert", None),
        P("expert", None),
        P("expert", None, "hsplit"),
        P("expert", None, "hsplit"),
        P("expert", "hsplit", None),
    )
    return jax.shard_map(
        local, mesh=mesh, in_specs=placed, out_specs=P("expert", "hsplit"), check_vma=False
    )
```

```python
import jax
import jax.numpy as jnp
from jax import lax
from jax.experimental import pallas as pl
from jax.experimental.pallas import tpu as pltpu
from jax.sharding import PartitionSpec as P

EXPERTS = 16
Q = 4
Z = 8
TOP = 8
LX = 4
LY = 4
TOK = 16
D = 7168
W = D // Q
PART = 384
REST = W - 2 * PART
PIECE = W // Z
UNITS = 256
ROWS = EXPERTS * TOK
SUB = ROWS // 2
SHARE = ROWS // Q
BF = jnp.bfloat16
F32 = jnp.float32


def kernel(
    tok_in, routes_in, rw_in, gate_in, up_in, down_in, out,
    tok, routes, rw, xb, bb, wg, wu, wd, dj, acc, pbuf, pcore, ybuf, py, hid,
    fmat, wbuf, zs, zr, fin, ret, tx1, rx1, tx2, rx2, ty, ry, tz, rz,
    w_sem, g_send, g_recv, b_send, b_recv, x_send, x_recv, y_send, y_recv, bx_send, bx_recv,
    up_send, up_recv, dn_send, dn_recv,
    p_send, p_recv, m_send, m_recv, h_send, h_recv, z_send, z_recv, a_send, a_recv,
    f_send, f_recv, r1_send, r1_recv, r2_send, r2_recv, ry_send, ry_recv, rz_send, rz_recv,
):
    p = lax.axis_index("expert")
    z = lax.axis_index("hsplit")
    e, q = p // Q, p % Q
    ex, ey = e // LY, e % LY
    z_up, z_dn = (z + 1) % Z, (z + Z - 1) % Z
    open_sends = []

    def remote(src, dst, send, recv, to_p, to_z):
        return pltpu.make_async_remote_copy(
            src_ref=src, dst_ref=dst, send_sem=send, recv_sem=recv,
            device_id=(to_p, to_z), device_id_type=pl.DeviceIdType.MESH,
        )

    def send(*args):
        copy = remote(*args)
        copy.start()
        open_sends.append(copy)

    def arrived(ref, sem):
        pltpu.make_async_copy(ref, ref, sem).wait()

    def owner(x, y, k):
        return (x * LY + y) * Q + k

    def rows(start, count):
        return pl.ds(pl.multiple_of(start, 16), count)

    pairs = ((tok_in, tok), (routes_in, routes), (rw_in, rw), (gate_in, wg), (up_in, wu), (down_in, wd))
    loads = [pltpu.make_async_copy(src, dst, w_sem.at[i]) for i, (src, dst) in enumerate(pairs)]
    for load in loads:
        load.start()

    barrier = pltpu.get_barrier_semaphore()

    def greet(i, carry):
        pl.semaphore_signal(
            barrier, inc=1, device_id=((p + i) % (EXPERTS * Q), z), device_id_type=pl.DeviceIdType.MESH
        )
        return carry

    lax.fori_loop(1, EXPERTS * Q, greet, 0)

    def greet_z(i, carry):
        pl.semaphore_signal(
            barrier, inc=1, device_id=(e * Q + i % Q, (z + i // Q) % Z), device_id_type=pl.DeviceIdType.MESH
        )
        return carry

    lax.fori_loop(Q, Z * Q, greet_z, 0)
    loads[0].wait()
    pl.semaphore_wait(barrier, EXPERTS * Q - 1 + (Z - 1) * Q)

    side = jnp.where(z % 2 == 1, 1, Q - 1)
    own_group = z // 2
    order = (own_group, (own_group + side) % Q, (own_group + 2 * Q - side) % Q, (own_group + 2) % Q)
    column = LY * TOK
    own_rows = rows(e * TOK, TOK)

    mine = xb.at[z, own_rows]
    shares = q == z // 2

    def share_of(to_q):
        return tok.at[:, pl.ds(pl.multiple_of(to_q * W + (z % 2) * PART, 128), PART)]

    g_copies = [
        remote(
            share_of((q + d % Q) % Q), mine, g_send.at[d], g_recv.at[0],
            owner(ex, (ey + d // Q) % LY, (q + d % Q) % Q), z,
        )
        for d in range(1, Q * LY)
    ]
    own_share = pltpu.make_async_copy(share_of(q), mine, g_recv.at[0])

    def rest_of(to_q):
        return tok.at[:, pl.ds(pl.multiple_of(to_q * W + 2 * PART, 128), REST)]

    own_rest = pltpu.make_async_copy(rest_of(q), bb.at[q, own_rows], b_recv.at[0])
    for d in range(1, Q):
        to = (q + d) % Q
        send(rest_of(to), bb.at[q, own_rows], b_send.at[d], b_recv.at[d], e * Q + to, z)
    own_rest.start()

    @pl.when(shares)
    def _():
        for copy in g_copies:
            copy.start()
        own_share.start()

    own_rest.wait()
    for d in range(1, Q):
        arrived(bb.at[(q + Q - d) % Q, own_rows], b_recv.at[d])

    def y_sends(i):
        ref = bb.at[order[i], own_rows]
        for d in (1, 3, 2):
            send(ref, ref, y_send.at[i, d], y_recv.at[i, d], owner(ex, (ey + d) % LY, q), z)

    def y_arrived(i):
        for d in (1, 3, 2):
            arrived(bb.at[order[i], rows((ex * LY + (ey + LY - d) % LY) * TOK, TOK)], y_recv.at[i, d])

    x_up, x_dn = (ex + 1) % LX, (ex + LX - 1) % LX
    x_far = (ex + 2) % LX

    def x_sends(i):
        ref = bb.at[order[i], rows(ex * column, column)]
        send(ref, ref, bx_send.at[i, 0], bx_recv.at[i, 0], owner(x_up, ey, q), z)
        send(ref, ref, bx_send.at[i, 1], bx_recv.at[i, 1], owner(x_dn, ey, q), z)

    def x_forward(i):
        half = column // 2
        arrived(bb.at[order[i], rows(x_dn * column, column)], bx_recv.at[i, 0])
        ref = bb.at[order[i], rows(x_dn * column, half)]
        send(ref, ref, bx_send.at[i, 2], bx_recv.at[i, 2], owner(x_up, ey, q), z)
        arrived(bb.at[order[i], rows(x_up * column, column)], bx_recv.at[i, 1])
        ref = bb.at[order[i], rows(x_up * column + half, half)]
        send(ref, ref, bx_send.at[i, 3], bx_recv.at[i, 3], owner(x_dn, ey, q), z)

    def x_arrived(i):
        half = column // 2
        arrived(bb.at[order[i], rows(x_far * column, half)], bx_recv.at[i, 2])
        arrived(bb.at[order[i], rows(x_far * column + half, half)], bx_recv.at[i, 3])

    y_sends(0)
    mine_x = xb.at[z, rows(ex * column, column)]
    arrived(mine_x, g_recv.at[0])
    for d in range(1, LX):
        send(mine_x, mine_x, x_send.at[d], x_recv.at[d], owner((ex + d) % LX, ey, q), z)
    for i in range(1, Q):
        y_sends(i)

    y_arrived(0)
    x_sends(0)
    for d in range(1, LX):
        arrived(xb.at[z, rows(((ex + LX - d) % LX) * column, column)], x_recv.at[d])

    steps = 7

    def half_of(block, k, way):
        which = k % 2 if way > 0 else (k + 1) % 2
        return xb.at[block, pl.ds(which * SUB, SUB)]

    def ring_send(k, way):
        block = (z - way * (k // 2) + Z) % Z
        ref = half_of(block, k, way)
        if way > 0:
            send(ref, ref, up_send.at[k], up_recv.at[k], p, z_up)
        else:
            send(ref, ref, dn_send.at[k], dn_recv.at[k], p, z_dn)

    def ring_step(k):
        for way in (1, -1):
            block = (z - way * (k // 2 + 1) + 2 * Z) % Z
            arrived(half_of(block, k, way), (up_recv if way > 0 else dn_recv).at[k])
            if k + 2 < steps:
                ring_send(k + 2, way)

    def add_terms(group, x, wrows, first):
        for at, w in ((0, wg), (UNITS, wu)):
            value = jnp.dot(x, w[wrows, :], preferred_element_type=F32)
            if first:
                acc[group, :, at : at + UNITS] = value
            else:
                acc[group, :, at : at + UNITS] += value

    def add_block(block, first):
        add_terms(block // 2, xb[block], pl.ds(pl.multiple_of((block % 2) * PART, 128), PART), first)

    def add_rest(i):
        x_arrived(i)
        add_terms(order[i], bb[order[i]], pl.ds(2 * PART, REST), False)

    core, chip = q % 2, q // 2

    def share_row(k):
        return (k % 2) * 2 * SHARE + (k // 2) * SHARE

    def share_partials(i):
        pbuf[i] = acc[order[i], rows((1 - core) * 2 * SHARE, 2 * SHARE), :].astype(BF)
        send(pbuf.at[i], pcore.at[i], p_send.at[i], p_recv.at[i], e * Q + chip * 2 + 1 - core, z)

    def cross(i):
        far, near = rows((1 - chip) * SHARE, SHARE), rows(chip * SHARE, SHARE)
        far_row = core * 2 * SHARE + (1 - chip) * SHARE
        arrived(pcore.at[i], p_recv.at[i])
        ybuf[i] = (acc[order[i], rows(far_row, SHARE), :] + pcore[i, far, :].astype(F32)).astype(BF)
        send(ybuf.at[i], py.at[i], m_send.at[i], m_recv.at[i], e * Q + (1 - chip) * 2 + core, z)
        acc[order[i], rows(share_row(q), SHARE), :] += pcore[i, near, :].astype(F32)

    def share_hidden(i):
        here = rows(share_row(q), SHARE)
        arrived(py.at[i], m_recv.at[i])
        total = acc[order[i], here, :] + py[i].astype(F32)
        g, u = total[:, :UNITS], total[:, UNITS:]
        if i == 0:
            arrived(wbuf, f_recv.at[0])
        factor = wbuf[order[i]].reshape(SHARE, 128)
        at_expert = lax.broadcasted_iota(jnp.int32, (SHARE, 128), 1) == e
        factor = jnp.sum(jnp.where(at_expert, factor, 0.0), axis=1, keepdims=True)
        hid[order[i], here, :] = (g / (1.0 + jnp.exp(-g)) * u * factor).astype(BF)
        ref = hid.at[order[i], here]
        for d in range(1, Q):
            send(ref, ref, h_send.at[i, d], h_recv.at[i, d], e * Q + (q + d) % Q, z)

    even = z % 2 == 0

    def nth(up, down):
        return jnp.where(even, (z + up) % Z, (z + down) % Z)

    for k in (0, 1):
        ring_send(k, 1)
        ring_send(k, -1)
    for load in loads[1:]:
        load.wait()

    named, share = routes[...], rw[...]
    lane = lax.broadcasted_iota(jnp.int32, (TOK, TOK), 1)
    diagonal = lane == lax.broadcasted_iota(jnp.int32, (TOK, TOK), 0)
    wide = lax.broadcasted_iota(jnp.int32, (TOK, 128), 1)
    factors = jnp.zeros((TOK, 128), F32)
    for x in range(EXPERTS):
        row = jnp.sum(jnp.where(named == x, share, 0.0), axis=0, keepdims=True)
        factor = jnp.sum(jnp.where(diagonal, row, 0.0), axis=1, keepdims=True)
        factors = jnp.where(wide == x, factor, factors)
    fmat[...] = factors


    def share_factors(i, carry):
        to = (e + i) % EXPERTS * Q + share_of_column

        @pl.when(to != p)
        def _():
            remote(fmat, wbuf.at[q, ey], f_send.at[i], f_recv.at[0], to, z).start()

        @pl.when(to == p)
        def _():
            pltpu.make_async_copy(fmat, wbuf.at[q, ey], f_recv.at[0]).start()

        return carry

    share_of_column = (ex % 2) * 2 + ex // 2
    lax.fori_loop(0, EXPERTS, share_factors, 0)
    add_block(z, True)
    for j in range(Z):
        dj[j] = wd[:, j * PIECE : (j + 1) * PIECE]
    y_arrived(1)
    x_sends(1)
    ring_step(0)
    x_forward(0)
    ring_step(1)
    add_block(nth(1, Z - 1), False)
    add_rest(0)
    share_partials(0)
    y_arrived(2)
    x_sends(2)
    ring_step(2)
    x_forward(1)
    add_block(nth(Z - 1, 1), True)
    cross(0)
    ring_step(3)
    add_block(nth(Z - 2, 2), False)
    add_rest(1)
    share_partials(1)
    share_hidden(0)
    y_arrived(3)
    x_sends(3)
    ring_step(4)
    x_forward(2)
    add_block(nth(2, Z - 2), True)
    cross(1)
    ring_step(5)
    add_block(nth(3, Z - 3), False)
    add_rest(2)
    share_partials(2)
    share_hidden(1)
    x_forward(3)
    add_block(nth(Z - 3, 3), True)
    cross(2)
    ring_step(6)
    add_block((z + 4) % Z, False)
    share_hidden(2)
    add_rest(3)
    share_partials(3)
    cross(3)
    share_hidden(3)
    for i in range(Q):
        for d in range(1, Q):
            arrived(hid.at[order[i], rows(share_row((q + Q - d) % Q), SHARE)], h_recv.at[i, d])

    def z_part(ref, g, w, s, part):
        return ref.at[g, w, s, part * SUB : (part + 1) * SUB]

    def z_copy(g, w, s, part):
        return remote(
            z_part(zs, g, w, s, part), z_part(zr, g, w, s, part), z_send.at[g, w, s, part],
            z_recv.at[g, w, s, part], p, z_dn if w else z_up,
        )

    def term(g, part, j):
        return jnp.dot(hid[g, part * SUB : (part + 1) * SUB, :], dj[j], preferred_element_type=F32)

    def z_step(g, s):
        for turn in (0, 1):
            for w in (0, 1):
                part = turn if w == 0 else 1 - turn
                if s == 0 and part != w:
                    continue
                j = (z + (4 - s) * (1 - 2 * w) + Z) % Z
                value = term(g, part, j)
                if s > 1 or (s == 1 and part == w):
                    arrived(z_part(zr, g, w, s - 1, part), z_recv.at[g, w, s - 1, part])
                    value += zr[g, w, s - 1, part * SUB : (part + 1) * SUB, :].astype(F32)
                zs[g, w, s, part * SUB : (part + 1) * SUB, :] = value.astype(BF)
                z_copy(g, w, s, part).start()

    def z_last(g):
        for part in (0, 1):
            value = term(g, part, z)
            for w in (0, 1):
                arrived(z_part(zr, g, w, 3, part), z_recv.at[g, w, 3, part])
                value += zr[g, w, 3, part * SUB : (part + 1) * SUB, :].astype(F32)
            fin[g, part * SUB : (part + 1) * SUB, :] = value.astype(BF)

        def home(i, carry):
            to_e = (e + i) % EXPERTS
            to = to_e * Q + g
            src = fin.at[g, rows(to_e * TOK, TOK)]

            @pl.when(to != p)
            def _():
                remote(src, ret.at[p], a_send.at[0], a_recv.at[0], to, z).start()

            @pl.when(to == p)
            def _():
                pltpu.make_async_copy(src, ret.at[p], a_recv.at[0]).start()

            return carry

        lax.fori_loop(0, EXPERTS, home, 0)

    half = column // 2

    def full_term(t, x):
        return jnp.dot(hid[2 + t, rows(x * column, column), :], wd[...], preferred_element_type=F32)

    def plane_far(t):
        tx1[t] = full_term(t, x_far).astype(BF)
        send(tx1.at[t, :half], rx1.at[t, 0], r1_send.at[t, 0], r1_recv.at[t, 0], owner(x_up, ey, q), z)
        send(tx1.at[t, half:], rx1.at[t, 1], r1_send.at[t, 1], r1_recv.at[t, 1], owner(x_dn, ey, q), z)

    def plane_near(t):
        for w, x in ((0, x_up), (1, x_dn)):
            value = full_term(t, x)
            mid, rest = slice(w * half, w * half + half), slice((1 - w) * half, (1 - w) * half + half)
            tx2[t, w, rest, :] = value[rest].astype(BF)
            arrived(rx1.at[t, w], r1_recv.at[t, w])
            tx2[t, w, mid, :] = (value[mid] + rx1[t, w].astype(F32)).astype(BF)
            send(tx2.at[t, w], rx2.at[t, w], r2_send.at[t, w], r2_recv.at[t, w], owner(x, ey, q), z)

    def plane_y(t):
        value = full_term(t, ex)
        for w in (0, 1):
            arrived(rx2.at[t, w], r2_recv.at[t, w])
            value += rx2[t, w].astype(F32)
        ty[t] = value.astype(BF)
        for d in (1, 3, 2):
            to = (ey + d) % LY
            send(
                ty.at[t, rows(to * TOK, TOK)], ry.at[t, d - 1], ry_send.at[t, d - 1], ry_recv.at[t, d - 1],
                owner(ex, to, q), z,
            )

    def home_copy(t, j):
        return remote(tz.at[t, j], rz.at[q, z], rz_send.at[t, j], rz_recv.at[0], e * Q + 2 + t, j)

    def is_here(t, j):
        return jnp.logical_and(q == 2 + t, z == j)

    def plane_home(t):
        value = ty[t, rows(ey * TOK, TOK), :].astype(F32)
        for d in (1, 3, 2):
            arrived(ry.at[t, d - 1], ry_recv.at[t, d - 1])
            value += ry[t, d - 1].astype(F32)
        for j in range(Z):
            tz[t, j] = value[:, j * PIECE : (j + 1) * PIECE].astype(BF)
        for j in range(Z):

            @pl.when(jnp.logical_not(is_here(t, j)))
            def _(j=j):
                home_copy(t, j).start()

            @pl.when(is_here(t, j))
            def _(j=j):
                pltpu.make_async_copy(tz.at[t, j], rz.at[q, z], rz_recv.at[0]).start()

    z_step(0, 0)
    z_step(1, 0)
    plane_far(0)
    plane_far(1)
    z_step(0, 1)
    z_step(1, 1)
    plane_near(0)
    z_step(0, 2)
    plane_near(1)
    z_step(1, 2)
    plane_y(0)
    z_step(0, 3)
    z_step(1, 3)
    plane_y(1)
    z_last(0)
    plane_home(0)
    z_last(1)
    plane_home(1)

    @pl.when(q < 2)
    def _():
        arrived(ret, a_recv.at[0])
        for k in range(Q):
            total = ret[k].astype(F32)
            for x in range(1, EXPERTS):
                total += ret[x * Q + k].astype(F32)
            out[k] = total.astype(BF)
        arrived(ret.at[pl.ds(0, 2 * EXPERTS - 1)], a_send.at[0])

    @pl.when(q >= 2)
    def _():
        arrived(rz, rz_recv.at[0])
        for k in range(Q):
            total = rz[k, 0].astype(F32)
            for j in range(1, Z):
                total += rz[k, j].astype(F32)
            out[k] = total.astype(BF)
        arrived(ret.at[pl.ds(0, 2 * EXPERTS)], a_send.at[0])

    for copy in open_sends:
        copy.wait_send()

    @pl.when(shares)
    def _():
        for copy in g_copies:
            copy.wait_send()

    def factors_sent(i, carry):
        to = (e + i) % EXPERTS * Q + share_of_column

        @pl.when(to != p)
        def _():
            remote(fmat, wbuf.at[q, ey], f_send.at[i], f_recv.at[0], to, z).wait_send()

        return carry

    lax.fori_loop(0, EXPERTS, factors_sent, 0)
    for g in range(2):
        for w in range(2):
            for s in range(4):
                for part in range(2):
                    if s > 0 or part == w:
                        z_copy(g, w, s, part).wait_send()
    for t in range(2):
        for j in range(Z):

            @pl.when(jnp.logical_not(is_here(t, j)))
            def _(t=t, j=j):
                home_copy(t, j).wait_send()


def local(tokens, routes, route_weights, gate_weight, up_weight, down_weight):
    dma = pltpu.SemaphoreType.DMA
    vmem = pl.BlockSpec(memory_space=pltpu.VMEM)
    anywhere = pl.BlockSpec(memory_space=pl.ANY)
    got = pl.pallas_call(
        kernel,
        out_shape=jax.ShapeDtypeStruct((Q, TOK, PIECE), BF),
        in_specs=[anywhere] * 6,
        out_specs=vmem,
        scratch_shapes=[
            pltpu.VMEM((TOK, D), BF),
            pltpu.VMEM((TOP, TOK), jnp.int32),
            pltpu.VMEM((TOP, TOK), F32),
            pltpu.VMEM((Z, ROWS, PART), BF),
            pltpu.VMEM((Q, ROWS, REST), BF),
            pltpu.VMEM((W, UNITS), BF),
            pltpu.VMEM((W, UNITS), BF),
            pltpu.VMEM((UNITS, W), BF),
            pltpu.VMEM((Z, UNITS, PIECE), BF),
            pltpu.VMEM((Q, ROWS, 2 * UNITS), F32),
            pltpu.VMEM((Q, 2 * SHARE, 2 * UNITS), BF),
            pltpu.VMEM((Q, 2 * SHARE, 2 * UNITS), BF),
            pltpu.VMEM((Q, SHARE, 2 * UNITS), BF),
            pltpu.VMEM((Q, SHARE, 2 * UNITS), BF),
            pltpu.VMEM((Q, ROWS, UNITS), BF),
            pltpu.VMEM((TOK, 128), F32),
            pltpu.VMEM((Q, LY, TOK, 128), F32),
            pltpu.VMEM((2, 2, 4, ROWS, PIECE), BF),
            pltpu.VMEM((2, 2, 4, ROWS, PIECE), BF),
            pltpu.VMEM((2, ROWS, PIECE), BF),
            pltpu.VMEM((EXPERTS * Q, TOK, PIECE), BF),
            pltpu.VMEM((2, SHARE, W), BF),
            pltpu.VMEM((2, 2, SHARE // 2, W), BF),
            pltpu.VMEM((2, 2, SHARE, W), BF),
            pltpu.VMEM((2, 2, SHARE, W), BF),
            pltpu.VMEM((2, SHARE, W), BF),
            pltpu.VMEM((2, LY - 1, TOK, W), BF),
            pltpu.VMEM((2, Z, TOK, PIECE), BF),
            pltpu.VMEM((Q, Z, TOK, PIECE), BF),
            dma((6,)), dma((16,)), dma((1,)), dma((4,)), dma((4,)), dma((4,)), dma((4,)),
            dma((4, 4)), dma((4, 4)), dma((4, 4)), dma((4, 4)),
            dma((7,)), dma((7,)), dma((7,)), dma((7,)),
            dma((4,)), dma((4,)), dma((4,)), dma((4,)), dma((4, 4)), dma((4, 4)),
            dma((2, 2, 4, 2)), dma((2, 2, 4, 2)), dma((1,)), dma((1,)),
            dma((16,)), dma((1,)), dma((2, 2)), dma((2, 2)), dma((2, 2)), dma((2, 2)),
            dma((2, 3)), dma((2, 3)), dma((2, 8)), dma((1,)),
        ],
        compiler_params=pltpu.CompilerParams(
            collective_id=0, has_side_effects=True, vmem_limit_bytes=60 * 1024 * 1024
        ),
        cost_estimate=pl.CostEstimate(flops=3 * 10**9, bytes_accessed=4 * 10**6, transcendentals=10**5),
    )(tokens, routes.T, route_weights.T, gate_weight[0], up_weight[0], down_weight[0])
    return got.transpose(1, 0, 2).reshape(TOK, Q * PIECE)


def solution(mesh):
    placed = (
        P("expert", None),
        P("expert", None),
        P("expert", None),
        P("expert", None, "hsplit"),
        P("expert", None, "hsplit"),
        P("expert", "hsplit", None),
    )
    return jax.shard_map(
        local, mesh=mesh, in_specs=placed, out_specs=P("expert", "hsplit"), check_vma=False
    )
```

```python
import jax
import jax.numpy as jnp
from jax import lax
from jax.experimental import pallas as pl
from jax.experimental.pallas import tpu as pltpu
from jax.sharding import PartitionSpec as P

EXPERTS = 16
Q = 4
Z = 8
TOP = 8
LX = 4
LY = 4
TOK = 16
D = 7168
W = D // Q
PART = 512
REST = W - 2 * PART
PIECE = W // Z
UNITS = 256
ROWS = EXPERTS * TOK
SUB = ROWS // 2
SHARE = ROWS // Q
BF = jnp.bfloat16
F32 = jnp.float32


def kernel(
    tok_in, routes_in, rw_in, gate_in, up_in, down_in, out,
    tok, routes, rw, xb, bb, wg, wu, wd, dj, acc, pbuf, pcore, ybuf, py, hid,
    fmat, wbuf, zs, zr, fin, ret, tx1, rx1, tx2, rx2, ty, ry, tz, rz,
    w_sem, g_send, g_recv, b_send, b_recv, x_send, x_recv, y_send, y_recv, bx_send, bx_recv,
    up_send, up_recv, dn_send, dn_recv,
    p_send, p_recv, m_send, m_recv, h_send, h_recv, z_send, z_recv, a_send, a_recv,
    f_send, f_recv, r1_send, r1_recv, r2_send, r2_recv, ry_send, ry_recv, rz_send, rz_recv,
):
    p = lax.axis_index("expert")
    z = lax.axis_index("hsplit")
    e, q = p // Q, p % Q
    ex, ey = e // LY, e % LY
    z_up, z_dn = (z + 1) % Z, (z + Z - 1) % Z
    open_sends = []

    def remote(src, dst, send, recv, to_p, to_z):
        return pltpu.make_async_remote_copy(
            src_ref=src, dst_ref=dst, send_sem=send, recv_sem=recv,
            device_id=(to_p, to_z), device_id_type=pl.DeviceIdType.MESH,
        )

    def send(*args):
        copy = remote(*args)
        copy.start()
        open_sends.append(copy)

    def arrived(ref, sem):
        pltpu.make_async_copy(ref, ref, sem).wait()

    def owner(x, y, k):
        return (x * LY + y) * Q + k

    def rows(start, count):
        return pl.ds(pl.multiple_of(start, 16), count)

    pairs = ((tok_in, tok), (routes_in, routes), (rw_in, rw), (gate_in, wg), (up_in, wu), (down_in, wd))
    loads = [pltpu.make_async_copy(src, dst, w_sem.at[i]) for i, (src, dst) in enumerate(pairs)]
    for load in loads:
        load.start()

    barrier = pltpu.get_barrier_semaphore()

    def greet(i, carry):
        pl.semaphore_signal(
            barrier, inc=1, device_id=((p + i) % (EXPERTS * Q), z), device_id_type=pl.DeviceIdType.MESH
        )
        return carry

    lax.fori_loop(1, EXPERTS * Q, greet, 0)

    def greet_z(i, carry):
        pl.semaphore_signal(
            barrier, inc=1, device_id=(e * Q + i % Q, (z + i // Q) % Z), device_id_type=pl.DeviceIdType.MESH
        )
        return carry

    lax.fori_loop(Q, Z * Q, greet_z, 0)
    loads[0].wait()
    pl.semaphore_wait(barrier, EXPERTS * Q - 1 + (Z - 1) * Q)

    side = jnp.where(z % 2 == 1, 1, Q - 1)
    own_group = z // 2
    order = (own_group, (own_group + side) % Q, (own_group + 2 * Q - side) % Q, (own_group + 2) % Q)
    column = LY * TOK
    own_rows = rows(e * TOK, TOK)

    mine = xb.at[z, own_rows]
    shares = q == z // 2

    def share_of(to_q):
        return tok.at[:, pl.ds(pl.multiple_of(to_q * W + (z % 2) * PART, 128), PART)]

    g_copies = [
        remote(
            share_of((q + d % Q) % Q), mine, g_send.at[d], g_recv.at[0],
            owner(ex, (ey + d // Q) % LY, (q + d % Q) % Q), z,
        )
        for d in range(1, Q * LY)
    ]
    own_share = pltpu.make_async_copy(share_of(q), mine, g_recv.at[0])

    def rest_of(to_q):
        return tok.at[:, pl.ds(pl.multiple_of(to_q * W + 2 * PART, 128), REST)]

    own_rest = pltpu.make_async_copy(rest_of(q), bb.at[q, own_rows], b_recv.at[0])
    for d in range(1, Q):
        to = (q + d) % Q
        send(rest_of(to), bb.at[q, own_rows], b_send.at[d], b_recv.at[d], e * Q + to, z)
    own_rest.start()

    @pl.when(shares)
    def _():
        for copy in g_copies:
            copy.start()
        own_share.start()

    own_rest.wait()
    for d in range(1, Q):
        arrived(bb.at[(q + Q - d) % Q, own_rows], b_recv.at[d])

    def y_sends(i):
        ref = bb.at[order[i], own_rows]
        for d in (1, 3, 2):
            send(ref, ref, y_send.at[i, d], y_recv.at[i, d], owner(ex, (ey + d) % LY, q), z)

    def y_arrived(i):
        for d in (1, 3, 2):
            arrived(bb.at[order[i], rows((ex * LY + (ey + LY - d) % LY) * TOK, TOK)], y_recv.at[i, d])

    x_up, x_dn = (ex + 1) % LX, (ex + LX - 1) % LX
    x_far = (ex + 2) % LX

    def x_sends(i):
        ref = bb.at[order[i], rows(ex * column, column)]
        send(ref, ref, bx_send.at[i, 0], bx_recv.at[i, 0], owner(x_up, ey, q), z)
        send(ref, ref, bx_send.at[i, 1], bx_recv.at[i, 1], owner(x_dn, ey, q), z)

    def x_forward(i):
        half = column // 2
        arrived(bb.at[order[i], rows(x_dn * column, column)], bx_recv.at[i, 0])
        ref = bb.at[order[i], rows(x_dn * column, half)]
        send(ref, ref, bx_send.at[i, 2], bx_recv.at[i, 2], owner(x_up, ey, q), z)
        arrived(bb.at[order[i], rows(x_up * column, column)], bx_recv.at[i, 1])
        ref = bb.at[order[i], rows(x_up * column + half, half)]
        send(ref, ref, bx_send.at[i, 3], bx_recv.at[i, 3], owner(x_dn, ey, q), z)

    def x_arrived(i):
        half = column // 2
        arrived(bb.at[order[i], rows(x_far * column, half)], bx_recv.at[i, 2])
        arrived(bb.at[order[i], rows(x_far * column + half, half)], bx_recv.at[i, 3])

    y_sends(0)
    mine_x = xb.at[z, rows(ex * column, column)]
    arrived(mine_x, g_recv.at[0])
    for d in range(1, LX):
        send(mine_x, mine_x, x_send.at[d], x_recv.at[d], owner((ex + d) % LX, ey, q), z)
    for i in range(1, Q):
        y_sends(i)

    y_arrived(0)
    x_sends(0)
    for d in range(1, LX):
        arrived(xb.at[z, rows(((ex + LX - d) % LX) * column, column)], x_recv.at[d])

    steps = 7

    def half_of(block, k, way):
        which = k % 2 if way > 0 else (k + 1) % 2
        return xb.at[block, pl.ds(which * SUB, SUB)]

    def ring_send(k, way):
        block = (z - way * (k // 2) + Z) % Z
        ref = half_of(block, k, way)
        if way > 0:
            send(ref, ref, up_send.at[k], up_recv.at[k], p, z_up)
        else:
            send(ref, ref, dn_send.at[k], dn_recv.at[k], p, z_dn)

    def ring_step(k):
        for way in (1, -1):
            block = (z - way * (k // 2 + 1) + 2 * Z) % Z
            arrived(half_of(block, k, way), (up_recv if way > 0 else dn_recv).at[k])
            if k + 2 < steps:
                ring_send(k + 2, way)

    def add_terms(group, x, wrows, first):
        for at, w in ((0, wg), (UNITS, wu)):
            value = jnp.dot(x, w[wrows, :], preferred_element_type=F32)
            if first:
                acc[group, :, at : at + UNITS] = value
            else:
                acc[group, :, at : at + UNITS] += value

    def add_block(block, first):
        add_terms(block // 2, xb[block], pl.ds(pl.multiple_of((block % 2) * PART, 128), PART), first)

    def add_rest(i):
        x_arrived(i)
        add_terms(order[i], bb[order[i]], pl.ds(2 * PART, REST), False)

    core, chip = q % 2, q // 2

    def share_row(k):
        return (k % 2) * 2 * SHARE + (k // 2) * SHARE

    def share_partials(i):
        pbuf[i] = acc[order[i], rows((1 - core) * 2 * SHARE, 2 * SHARE), :].astype(BF)
        send(pbuf.at[i], pcore.at[i], p_send.at[i], p_recv.at[i], e * Q + chip * 2 + 1 - core, z)

    def cross(i):
        far, near = rows((1 - chip) * SHARE, SHARE), rows(chip * SHARE, SHARE)
        far_row = core * 2 * SHARE + (1 - chip) * SHARE
        arrived(pcore.at[i], p_recv.at[i])
        ybuf[i] = (acc[order[i], rows(far_row, SHARE), :] + pcore[i, far, :].astype(F32)).astype(BF)
        send(ybuf.at[i], py.at[i], m_send.at[i], m_recv.at[i], e * Q + (1 - chip) * 2 + core, z)
        acc[order[i], rows(share_row(q), SHARE), :] += pcore[i, near, :].astype(F32)

    def share_hidden(i):
        here = rows(share_row(q), SHARE)
        arrived(py.at[i], m_recv.at[i])
        total = acc[order[i], here, :] + py[i].astype(F32)
        g, u = total[:, :UNITS], total[:, UNITS:]
        if i == 0:
            arrived(wbuf, f_recv.at[0])
        factor = wbuf[order[i]].reshape(SHARE, 128)
        at_expert = lax.broadcasted_iota(jnp.int32, (SHARE, 128), 1) == e
        factor = jnp.sum(jnp.where(at_expert, factor, 0.0), axis=1, keepdims=True)
        hid[order[i], here, :] = (g / (1.0 + jnp.exp(-g)) * u * factor).astype(BF)
        ref = hid.at[order[i], here]
        for d in range(1, Q):
            send(ref, ref, h_send.at[i, d], h_recv.at[i, d], e * Q + (q + d) % Q, z)

    even = z % 2 == 0

    def nth(up, down):
        return jnp.where(even, (z + up) % Z, (z + down) % Z)

    for k in (0, 1):
        ring_send(k, 1)
        ring_send(k, -1)
    for load in loads[1:]:
        load.wait()

    named, share = routes[...], rw[...]
    lane = lax.broadcasted_iota(jnp.int32, (TOK, TOK), 1)
    diagonal = lane == lax.broadcasted_iota(jnp.int32, (TOK, TOK), 0)
    wide = lax.broadcasted_iota(jnp.int32, (TOK, 128), 1)
    factors = jnp.zeros((TOK, 128), F32)
    for x in range(EXPERTS):
        row = jnp.sum(jnp.where(named == x, share, 0.0), axis=0, keepdims=True)
        factor = jnp.sum(jnp.where(diagonal, row, 0.0), axis=1, keepdims=True)
        factors = jnp.where(wide == x, factor, factors)
    fmat[...] = factors


    def share_factors(i, carry):
        to = (e + i) % EXPERTS * Q + share_of_column

        @pl.when(to != p)
        def _():
            remote(fmat, wbuf.at[q, ey], f_send.at[i], f_recv.at[0], to, z).start()

        @pl.when(to == p)
        def _():
            pltpu.make_async_copy(fmat, wbuf.at[q, ey], f_recv.at[0]).start()

        return carry

    share_of_column = (ex % 2) * 2 + ex // 2
    lax.fori_loop(0, EXPERTS, share_factors, 0)
    add_block(z, True)
    for j in range(Z):
        dj[j] = wd[:, j * PIECE : (j + 1) * PIECE]
    y_arrived(1)
    x_sends(1)
    ring_step(0)
    x_forward(0)
    ring_step(1)
    add_block(nth(1, Z - 1), False)
    add_rest(0)
    share_partials(0)
    y_arrived(2)
    x_sends(2)
    ring_step(2)
    x_forward(1)
    add_block(nth(Z - 1, 1), True)
    cross(0)
    ring_step(3)
    add_block(nth(Z - 2, 2), False)
    add_rest(1)
    share_partials(1)
    share_hidden(0)
    y_arrived(3)
    x_sends(3)
    ring_step(4)
    x_forward(2)
    add_block(nth(2, Z - 2), True)
    cross(1)
    ring_step(5)
    add_block(nth(3, Z - 3), False)
    add_rest(2)
    share_partials(2)
    share_hidden(1)
    x_forward(3)
    add_block(nth(Z - 3, 3), True)
    cross(2)
    ring_step(6)
    add_block((z + 4) % Z, False)
    share_hidden(2)
    add_rest(3)
    share_partials(3)
    cross(3)
    share_hidden(3)
    for i in range(Q):
        for d in range(1, Q):
            arrived(hid.at[order[i], rows(share_row((q + Q - d) % Q), SHARE)], h_recv.at[i, d])

    def z_part(ref, g, w, s, part):
        return ref.at[g, w, s, part * SUB : (part + 1) * SUB]

    def z_copy(g, w, s, part):
        return remote(
            z_part(zs, g, w, s, part), z_part(zr, g, w, s, part), z_send.at[g, w, s, part],
            z_recv.at[g, w, s, part], p, z_dn if w else z_up,
        )

    def term(g, part, j):
        return jnp.dot(hid[g, part * SUB : (part + 1) * SUB, :], dj[j], preferred_element_type=F32)

    def z_step(g, s):
        for turn in (0, 1):
            for w in (0, 1):
                part = turn if w == 0 else 1 - turn
                if s == 0 and part != w:
                    continue
                j = (z + (4 - s) * (1 - 2 * w) + Z) % Z
                value = term(g, part, j)
                if s > 1 or (s == 1 and part == w):
                    arrived(z_part(zr, g, w, s - 1, part), z_recv.at[g, w, s - 1, part])
                    value += zr[g, w, s - 1, part * SUB : (part + 1) * SUB, :].astype(F32)
                zs[g, w, s, part * SUB : (part + 1) * SUB, :] = value.astype(BF)
                z_copy(g, w, s, part).start()

    def z_last(g):
        for part in (0, 1):
            value = term(g, part, z)
            for w in (0, 1):
                arrived(z_part(zr, g, w, 3, part), z_recv.at[g, w, 3, part])
                value += zr[g, w, 3, part * SUB : (part + 1) * SUB, :].astype(F32)
            fin[g, part * SUB : (part + 1) * SUB, :] = value.astype(BF)

        def home(i, carry):
            to_e = (e + i) % EXPERTS
            to = to_e * Q + g
            src = fin.at[g, rows(to_e * TOK, TOK)]

            @pl.when(to != p)
            def _():
                remote(src, ret.at[p], a_send.at[0], a_recv.at[0], to, z).start()

            @pl.when(to == p)
            def _():
                pltpu.make_async_copy(src, ret.at[p], a_recv.at[0]).start()

            return carry

        lax.fori_loop(0, EXPERTS, home, 0)

    half = column // 2

    def full_term(t, x):
        return jnp.dot(hid[2 + t, rows(x * column, column), :], wd[...], preferred_element_type=F32)

    def plane_far(t):
        tx1[t] = full_term(t, x_far).astype(BF)
        send(tx1.at[t, :half], rx1.at[t, 0], r1_send.at[t, 0], r1_recv.at[t, 0], owner(x_up, ey, q), z)
        send(tx1.at[t, half:], rx1.at[t, 1], r1_send.at[t, 1], r1_recv.at[t, 1], owner(x_dn, ey, q), z)

    def plane_near(t):
        for w, x in ((0, x_up), (1, x_dn)):
            value = full_term(t, x)
            mid, rest = slice(w * half, w * half + half), slice((1 - w) * half, (1 - w) * half + half)
            tx2[t, w, rest, :] = value[rest].astype(BF)
            arrived(rx1.at[t, w], r1_recv.at[t, w])
            tx2[t, w, mid, :] = (value[mid] + rx1[t, w].astype(F32)).astype(BF)
            send(tx2.at[t, w], rx2.at[t, w], r2_send.at[t, w], r2_recv.at[t, w], owner(x, ey, q), z)

    def plane_y(t):
        value = full_term(t, ex)
        for w in (0, 1):
            arrived(rx2.at[t, w], r2_recv.at[t, w])
            value += rx2[t, w].astype(F32)
        ty[t] = value.astype(BF)
        for d in (1, 3, 2):
            to = (ey + d) % LY
            send(
                ty.at[t, rows(to * TOK, TOK)], ry.at[t, d - 1], ry_send.at[t, d - 1], ry_recv.at[t, d - 1],
                owner(ex, to, q), z,
            )

    def home_copy(t, j):
        return remote(tz.at[t, j], rz.at[q, z], rz_send.at[t, j], rz_recv.at[0], e * Q + 2 + t, j)

    def is_here(t, j):
        return jnp.logical_and(q == 2 + t, z == j)

    def plane_home(t):
        value = ty[t, rows(ey * TOK, TOK), :].astype(F32)
        for d in (1, 3, 2):
            arrived(ry.at[t, d - 1], ry_recv.at[t, d - 1])
            value += ry[t, d - 1].astype(F32)
        for j in range(Z):
            tz[t, j] = value[:, j * PIECE : (j + 1) * PIECE].astype(BF)
        for j in range(Z):

            @pl.when(jnp.logical_not(is_here(t, j)))
            def _(j=j):
                home_copy(t, j).start()

            @pl.when(is_here(t, j))
            def _(j=j):
                pltpu.make_async_copy(tz.at[t, j], rz.at[q, z], rz_recv.at[0]).start()

    plane_far(0)
    plane_far(1)
    z_step(0, 0)
    z_step(1, 0)
    plane_near(0)
    z_step(0, 1)
    z_step(1, 1)
    plane_near(1)
    z_step(0, 2)
    plane_y(0)
    z_step(1, 2)
    z_step(0, 3)
    plane_y(1)
    z_step(1, 3)
    plane_home(0)
    z_last(0)
    z_last(1)
    plane_home(1)

    @pl.when(q < 2)
    def _():
        arrived(ret, a_recv.at[0])
        for k in range(Q):
            total = ret[k].astype(F32)
            for x in range(1, EXPERTS):
                total += ret[x * Q + k].astype(F32)
            out[k] = total.astype(BF)
        arrived(ret.at[pl.ds(0, 2 * EXPERTS - 1)], a_send.at[0])

    @pl.when(q >= 2)
    def _():
        arrived(rz, rz_recv.at[0])
        for k in range(Q):
            total = rz[k, 0].astype(F32)
            for j in range(1, Z):
                total += rz[k, j].astype(F32)
            out[k] = total.astype(BF)
        arrived(ret.at[pl.ds(0, 2 * EXPERTS)], a_send.at[0])

    for copy in open_sends:
        copy.wait_send()

    @pl.when(shares)
    def _():
        for copy in g_copies:
            copy.wait_send()

    def factors_sent(i, carry):
        to = (e + i) % EXPERTS * Q + share_of_column

        @pl.when(to != p)
        def _():
            remote(fmat, wbuf.at[q, ey], f_send.at[i], f_recv.at[0], to, z).wait_send()

        return carry

    lax.fori_loop(0, EXPERTS, factors_sent, 0)
    for g in range(2):
        for w in range(2):
            for s in range(4):
                for part in range(2):
                    if s > 0 or part == w:
                        z_copy(g, w, s, part).wait_send()
    for t in range(2):
        for j in range(Z):

            @pl.when(jnp.logical_not(is_here(t, j)))
            def _(t=t, j=j):
                home_copy(t, j).wait_send()


def local(tokens, routes, route_weights, gate_weight, up_weight, down_weight):
    dma = pltpu.SemaphoreType.DMA
    vmem = pl.BlockSpec(memory_space=pltpu.VMEM)
    anywhere = pl.BlockSpec(memory_space=pl.ANY)
    got = pl.pallas_call(
        kernel,
        out_shape=jax.ShapeDtypeStruct((Q, TOK, PIECE), BF),
        in_specs=[anywhere] * 6,
        out_specs=vmem,
        scratch_shapes=[
            pltpu.VMEM((TOK, D), BF),
            pltpu.VMEM((TOP, TOK), jnp.int32),
            pltpu.VMEM((TOP, TOK), F32),
            pltpu.VMEM((Z, ROWS, PART), BF),
            pltpu.VMEM((Q, ROWS, REST), BF),
            pltpu.VMEM((W, UNITS), BF),
            pltpu.VMEM((W, UNITS), BF),
            pltpu.VMEM((UNITS, W), BF),
            pltpu.VMEM((Z, UNITS, PIECE), BF),
            pltpu.VMEM((Q, ROWS, 2 * UNITS), F32),
            pltpu.VMEM((Q, 2 * SHARE, 2 * UNITS), BF),
            pltpu.VMEM((Q, 2 * SHARE, 2 * UNITS), BF),
            pltpu.VMEM((Q, SHARE, 2 * UNITS), BF),
            pltpu.VMEM((Q, SHARE, 2 * UNITS), BF),
            pltpu.VMEM((Q, ROWS, UNITS), BF),
            pltpu.VMEM((TOK, 128), F32),
            pltpu.VMEM((Q, LY, TOK, 128), F32),
            pltpu.VMEM((2, 2, 4, ROWS, PIECE), BF),
            pltpu.VMEM((2, 2, 4, ROWS, PIECE), BF),
            pltpu.VMEM((2, ROWS, PIECE), BF),
            pltpu.VMEM((EXPERTS * Q, TOK, PIECE), BF),
            pltpu.VMEM((2, SHARE, W), BF),
            pltpu.VMEM((2, 2, SHARE // 2, W), BF),
            pltpu.VMEM((2, 2, SHARE, W), BF),
            pltpu.VMEM((2, 2, SHARE, W), BF),
            pltpu.VMEM((2, SHARE, W), BF),
            pltpu.VMEM((2, LY - 1, TOK, W), BF),
            pltpu.VMEM((2, Z, TOK, PIECE), BF),
            pltpu.VMEM((Q, Z, TOK, PIECE), BF),
            dma((6,)), dma((16,)), dma((1,)), dma((4,)), dma((4,)), dma((4,)), dma((4,)),
            dma((4, 4)), dma((4, 4)), dma((4, 4)), dma((4, 4)),
            dma((7,)), dma((7,)), dma((7,)), dma((7,)),
            dma((4,)), dma((4,)), dma((4,)), dma((4,)), dma((4, 4)), dma((4, 4)),
            dma((2, 2, 4, 2)), dma((2, 2, 4, 2)), dma((1,)), dma((1,)),
            dma((16,)), dma((1,)), dma((2, 2)), dma((2, 2)), dma((2, 2)), dma((2, 2)),
            dma((2, 3)), dma((2, 3)), dma((2, 8)), dma((1,)),
        ],
        compiler_params=pltpu.CompilerParams(
            collective_id=0, has_side_effects=True, vmem_limit_bytes=60 * 1024 * 1024
        ),
        cost_estimate=pl.CostEstimate(flops=3 * 10**9, bytes_accessed=4 * 10**6, transcendentals=10**5),
    )(tokens, routes.T, route_weights.T, gate_weight[0], up_weight[0], down_weight[0])
    return got.transpose(1, 0, 2).reshape(TOK, Q * PIECE)


def solution(mesh):
    placed = (
        P("expert", None),
        P("expert", None),
        P("expert", None),
        P("expert", None, "hsplit"),
        P("expert", None, "hsplit"),
        P("expert", "hsplit", None),
    )
    return jax.shard_map(
        local, mesh=mesh, in_specs=placed, out_specs=P("expert", "hsplit"), check_vma=False
    )
```

```python
import jax
import jax.numpy as jnp
from jax import lax
from jax.experimental import pallas as pl
from jax.experimental.pallas import tpu as pltpu
from jax.sharding import PartitionSpec as P

EXPERTS = 16
Q = 4
Z = 8
TOP = 8
LX = 4
LY = 4
TOK = 16
D = 7168
W = D // Q
PART = 512
REST = W - 2 * PART
PIECE = W // Z
UNITS = 256
ROWS = EXPERTS * TOK
SUB = ROWS // 2
SHARE = ROWS // Q
BF = jnp.bfloat16
F32 = jnp.float32


def kernel(
    tok_in, routes_in, rw_in, gate_in, up_in, down_in, out,
    tok, routes, rw, xb, bb, wg, wu, wd, dj, acc, pbuf, pcore, ybuf, py, hid,
    fmat, wbuf, zs, zr, fin, ret, tx1, rx1, tx2, rx2, ty, ry, tz, rz,
    w_sem, g_send, g_recv, b_send, b_recv, x_send, x_recv, y_send, y_recv, bx_send, bx_recv,
    up_send, up_recv, dn_send, dn_recv,
    p_send, p_recv, m_send, m_recv, h_send, h_recv, z_send, z_recv, a_send, a_recv,
    f_send, f_recv, r1_send, r1_recv, r2_send, r2_recv, ry_send, ry_recv, rz_send, rz_recv,
):
    p = lax.axis_index("expert")
    z = lax.axis_index("hsplit")
    e, q = p // Q, p % Q
    ex, ey = e // LY, e % LY
    z_up, z_dn = (z + 1) % Z, (z + Z - 1) % Z
    open_sends = []

    def remote(src, dst, send, recv, to_p, to_z):
        return pltpu.make_async_remote_copy(
            src_ref=src, dst_ref=dst, send_sem=send, recv_sem=recv,
            device_id=(to_p, to_z), device_id_type=pl.DeviceIdType.MESH,
        )

    def send(*args):
        copy = remote(*args)
        copy.start()
        open_sends.append(copy)

    def arrived(ref, sem):
        pltpu.make_async_copy(ref, ref, sem).wait()

    def owner(x, y, k):
        return (x * LY + y) * Q + k

    def rows(start, count):
        return pl.ds(pl.multiple_of(start, 16), count)

    pairs = ((tok_in, tok), (routes_in, routes), (rw_in, rw), (gate_in, wg), (up_in, wu), (down_in, wd))
    loads = [pltpu.make_async_copy(src, dst, w_sem.at[i]) for i, (src, dst) in enumerate(pairs)]
    for load in loads:
        load.start()

    barrier = pltpu.get_barrier_semaphore()

    def greet(i, carry):
        pl.semaphore_signal(
            barrier, inc=1, device_id=((p + i) % (EXPERTS * Q), z), device_id_type=pl.DeviceIdType.MESH
        )
        return carry

    lax.fori_loop(1, EXPERTS * Q, greet, 0)

    def greet_z(i, carry):
        pl.semaphore_signal(
            barrier, inc=1, device_id=(e * Q + i % Q, (z + i // Q) % Z), device_id_type=pl.DeviceIdType.MESH
        )
        return carry

    lax.fori_loop(Q, Z * Q, greet_z, 0)
    loads[0].wait()
    pl.semaphore_wait(barrier, EXPERTS * Q - 1 + (Z - 1) * Q)

    side = jnp.where(z % 2 == 1, 1, Q - 1)
    own_group = z // 2
    order = (own_group, (own_group + side) % Q, (own_group + 2 * Q - side) % Q, (own_group + 2) % Q)
    column = LY * TOK
    own_rows = rows(e * TOK, TOK)

    mine = xb.at[z, own_rows]
    shares = q == z // 2

    def share_of(to_q):
        return tok.at[:, pl.ds(pl.multiple_of(to_q * W + (z % 2) * PART, 128), PART)]

    g_copies = [
        remote(
            share_of((q + d % Q) % Q), mine, g_send.at[d], g_recv.at[0],
            owner(ex, (ey + d // Q) % LY, (q + d % Q) % Q), z,
        )
        for d in range(1, Q * LY)
    ]
    own_share = pltpu.make_async_copy(share_of(q), mine, g_recv.at[0])

    def rest_of(to_q):
        return tok.at[:, pl.ds(pl.multiple_of(to_q * W + 2 * PART, 128), REST)]

    own_rest = pltpu.make_async_copy(rest_of(q), bb.at[q, own_rows], b_recv.at[0])
    for d in range(1, Q):
        to = (q + d) % Q
        send(rest_of(to), bb.at[q, own_rows], b_send.at[d], b_recv.at[d], e * Q + to, z)
    own_rest.start()

    @pl.when(shares)
    def _():
        for copy in g_copies:
            copy.start()
        own_share.start()

    own_rest.wait()
    for d in range(1, Q):
        arrived(bb.at[(q + Q - d) % Q, own_rows], b_recv.at[d])

    def y_sends(i):
        ref = bb.at[order[i], own_rows]
        for d in (1, 3, 2):
            send(ref, ref, y_send.at[i, d], y_recv.at[i, d], owner(ex, (ey + d) % LY, q), z)

    def y_arrived(i):
        for d in (1, 3, 2):
            arrived(bb.at[order[i], rows((ex * LY + (ey + LY - d) % LY) * TOK, TOK)], y_recv.at[i, d])

    x_up, x_dn = (ex + 1) % LX, (ex + LX - 1) % LX
    x_far = (ex + 2) % LX

    def x_sends(i):
        ref = bb.at[order[i], rows(ex * column, column)]
        send(ref, ref, bx_send.at[i, 0], bx_recv.at[i, 0], owner(x_up, ey, q), z)
        send(ref, ref, bx_send.at[i, 1], bx_recv.at[i, 1], owner(x_dn, ey, q), z)

    def x_forward(i):
        half = column // 2
        arrived(bb.at[order[i], rows(x_dn * column, column)], bx_recv.at[i, 0])
        ref = bb.at[order[i], rows(x_dn * column, half)]
        send(ref, ref, bx_send.at[i, 2], bx_recv.at[i, 2], owner(x_up, ey, q), z)
        arrived(bb.at[order[i], rows(x_up * column, column)], bx_recv.at[i, 1])
        ref = bb.at[order[i], rows(x_up * column + half, half)]
        send(ref, ref, bx_send.at[i, 3], bx_recv.at[i, 3], owner(x_dn, ey, q), z)

    def x_arrived(i):
        half = column // 2
        arrived(bb.at[order[i], rows(x_far * column, half)], bx_recv.at[i, 2])
        arrived(bb.at[order[i], rows(x_far * column + half, half)], bx_recv.at[i, 3])

    y_sends(0)
    mine_x = xb.at[z, rows(ex * column, column)]
    arrived(mine_x, g_recv.at[0])
    for d in range(1, LX):
        send(mine_x, mine_x, x_send.at[d], x_recv.at[d], owner((ex + d) % LX, ey, q), z)
    for i in range(1, Q):
        y_sends(i)

    y_arrived(0)
    x_sends(0)
    for d in range(1, LX):
        arrived(xb.at[z, rows(((ex + LX - d) % LX) * column, column)], x_recv.at[d])

    steps = 7

    def half_of(block, k, way):
        which = k % 2 if way > 0 else (k + 1) % 2
        return xb.at[block, pl.ds(which * SUB, SUB)]

    def ring_send(k, way):
        block = (z - way * (k // 2) + Z) % Z
        ref = half_of(block, k, way)
        if way > 0:
            send(ref, ref, up_send.at[k], up_recv.at[k], p, z_up)
        else:
            send(ref, ref, dn_send.at[k], dn_recv.at[k], p, z_dn)

    def ring_step(k):
        for way in (1, -1):
            block = (z - way * (k // 2 + 1) + 2 * Z) % Z
            arrived(half_of(block, k, way), (up_recv if way > 0 else dn_recv).at[k])
            if k + 2 < steps:
                ring_send(k + 2, way)

    def add_terms(group, x, wrows, first):
        for at, w in ((0, wg), (UNITS, wu)):
            value = jnp.dot(x, w[wrows, :], preferred_element_type=F32)
            if first:
                acc[group, :, at : at + UNITS] = value
            else:
                acc[group, :, at : at + UNITS] += value

    def add_block(block, first):
        add_terms(block // 2, xb[block], pl.ds(pl.multiple_of((block % 2) * PART, 128), PART), first)

    def add_rest(i):
        x_arrived(i)
        add_terms(order[i], bb[order[i]], pl.ds(2 * PART, REST), False)

    core, chip = q % 2, q // 2

    def share_row(k):
        return (k % 2) * 2 * SHARE + (k // 2) * SHARE

    def share_partials(i):
        pbuf[i] = acc[order[i], rows((1 - core) * 2 * SHARE, 2 * SHARE), :].astype(BF)
        send(pbuf.at[i], pcore.at[i], p_send.at[i], p_recv.at[i], e * Q + chip * 2 + 1 - core, z)

    def cross(i):
        far, near = rows((1 - chip) * SHARE, SHARE), rows(chip * SHARE, SHARE)
        far_row = core * 2 * SHARE + (1 - chip) * SHARE
        arrived(pcore.at[i], p_recv.at[i])
        ybuf[i] = (acc[order[i], rows(far_row, SHARE), :] + pcore[i, far, :].astype(F32)).astype(BF)
        send(ybuf.at[i], py.at[i], m_send.at[i], m_recv.at[i], e * Q + (1 - chip) * 2 + core, z)
        acc[order[i], rows(share_row(q), SHARE), :] += pcore[i, near, :].astype(F32)

    def share_hidden(i):
        here = rows(share_row(q), SHARE)
        arrived(py.at[i], m_recv.at[i])
        total = acc[order[i], here, :] + py[i].astype(F32)
        g, u = total[:, :UNITS], total[:, UNITS:]
        if i == 0:
            arrived(wbuf, f_recv.at[0])
        factor = wbuf[order[i]].reshape(SHARE, 128)
        at_expert = lax.broadcasted_iota(jnp.int32, (SHARE, 128), 1) == e
        factor = jnp.sum(jnp.where(at_expert, factor, 0.0), axis=1, keepdims=True)
        hid[order[i], here, :] = (g / (1.0 + jnp.exp(-g)) * u * factor).astype(BF)
        ref = hid.at[order[i], here]
        for d in range(1, Q):
            send(ref, ref, h_send.at[i, d], h_recv.at[i, d], e * Q + (q + d) % Q, z)

    even = z % 2 == 0

    def nth(up, down):
        return jnp.where(even, (z + up) % Z, (z + down) % Z)

    for k in (0, 1):
        ring_send(k, 1)
        ring_send(k, -1)
    for load in loads[1:]:
        load.wait()

    named, share = routes[...], rw[...]
    lane = lax.broadcasted_iota(jnp.int32, (TOK, TOK), 1)
    diagonal = lane == lax.broadcasted_iota(jnp.int32, (TOK, TOK), 0)
    wide = lax.broadcasted_iota(jnp.int32, (TOK, 128), 1)
    factors = jnp.zeros((TOK, 128), F32)
    for x in range(EXPERTS):
        row = jnp.sum(jnp.where(named == x, share, 0.0), axis=0, keepdims=True)
        factor = jnp.sum(jnp.where(diagonal, row, 0.0), axis=1, keepdims=True)
        factors = jnp.where(wide == x, factor, factors)
    fmat[...] = factors


    def share_factors(i, carry):
        to = (e + i) % EXPERTS * Q + share_of_column

        @pl.when(to != p)
        def _():
            remote(fmat, wbuf.at[q, ey], f_send.at[i], f_recv.at[0], to, z).start()

        @pl.when(to == p)
        def _():
            pltpu.make_async_copy(fmat, wbuf.at[q, ey], f_recv.at[0]).start()

        return carry

    share_of_column = (ex % 2) * 2 + ex // 2
    lax.fori_loop(0, EXPERTS, share_factors, 0)
    add_block(z, True)
    for j in range(Z):
        dj[j] = wd[:, j * PIECE : (j + 1) * PIECE]
    y_arrived(1)
    x_sends(1)
    ring_step(0)
    x_forward(0)
    ring_step(1)
    add_block(nth(1, Z - 1), False)
    add_rest(0)
    share_partials(0)
    y_arrived(2)
    x_sends(2)
    ring_step(2)
    x_forward(1)
    add_block(nth(Z - 1, 1), True)
    cross(0)
    ring_step(3)
    add_block(nth(Z - 2, 2), False)
    add_rest(1)
    share_partials(1)
    share_hidden(0)
    y_arrived(3)
    x_sends(3)
    ring_step(4)
    x_forward(2)
    add_block(nth(2, Z - 2), True)
    cross(1)
    ring_step(5)
    add_block(nth(3, Z - 3), False)
    add_rest(2)
    share_partials(2)
    share_hidden(1)
    x_forward(3)
    add_block(nth(Z - 3, 3), True)
    cross(2)
    ring_step(6)
    add_block((z + 4) % Z, False)
    add_rest(3)
    share_partials(3)
    share_hidden(2)
    cross(3)
    share_hidden(3)
    for i in range(Q):
        for d in range(1, Q):
            arrived(hid.at[order[i], rows(share_row((q + Q - d) % Q), SHARE)], h_recv.at[i, d])

    def z_part(ref, g, w, s, part):
        return ref.at[g, w, s, part * SUB : (part + 1) * SUB]

    def z_copy(g, w, s, part):
        return remote(
            z_part(zs, g, w, s, part), z_part(zr, g, w, s, part), z_send.at[g, w, s, part],
            z_recv.at[g, w, s, part], p, z_dn if w else z_up,
        )

    def term(g, part, j):
        return jnp.dot(hid[g, part * SUB : (part + 1) * SUB, :], dj[j], preferred_element_type=F32)

    def z_step(g, s):
        for turn in (0, 1):
            for w in (0, 1):
                part = turn if w == 0 else 1 - turn
                if s == 0 and part != w:
                    continue
                j = (z + (4 - s) * (1 - 2 * w) + Z) % Z
                value = term(g, part, j)
                if s > 1 or (s == 1 and part == w):
                    arrived(z_part(zr, g, w, s - 1, part), z_recv.at[g, w, s - 1, part])
                    value += zr[g, w, s - 1, part * SUB : (part + 1) * SUB, :].astype(F32)
                zs[g, w, s, part * SUB : (part + 1) * SUB, :] = value.astype(BF)
                z_copy(g, w, s, part).start()

    def z_last(g):
        for part in (0, 1):
            value = term(g, part, z)
            for w in (0, 1):
                arrived(z_part(zr, g, w, 3, part), z_recv.at[g, w, 3, part])
                value += zr[g, w, 3, part * SUB : (part + 1) * SUB, :].astype(F32)
            fin[g, part * SUB : (part + 1) * SUB, :] = value.astype(BF)

        def home(i, carry):
            to_e = (e + i) % EXPERTS
            to = to_e * Q + g
            src = fin.at[g, rows(to_e * TOK, TOK)]

            @pl.when(to != p)
            def _():
                remote(src, ret.at[p], a_send.at[0], a_recv.at[0], to, z).start()

            @pl.when(to == p)
            def _():
                pltpu.make_async_copy(src, ret.at[p], a_recv.at[0]).start()

            return carry

        lax.fori_loop(0, EXPERTS, home, 0)

    half = column // 2

    def full_term(t, x):
        return jnp.dot(hid[2 + t, rows(x * column, column), :], wd[...], preferred_element_type=F32)

    def plane_far(t):
        tx1[t] = full_term(t, x_far).astype(BF)
        send(tx1.at[t, :half], rx1.at[t, 0], r1_send.at[t, 0], r1_recv.at[t, 0], owner(x_up, ey, q), z)
        send(tx1.at[t, half:], rx1.at[t, 1], r1_send.at[t, 1], r1_recv.at[t, 1], owner(x_dn, ey, q), z)

    def plane_near(t):
        for w, x in ((0, x_up), (1, x_dn)):
            value = full_term(t, x)
            mid, rest = slice(w * half, w * half + half), slice((1 - w) * half, (1 - w) * half + half)
            tx2[t, w, rest, :] = value[rest].astype(BF)
            arrived(rx1.at[t, w], r1_recv.at[t, w])
            tx2[t, w, mid, :] = (value[mid] + rx1[t, w].astype(F32)).astype(BF)
            send(tx2.at[t, w], rx2.at[t, w], r2_send.at[t, w], r2_recv.at[t, w], owner(x, ey, q), z)

    def plane_y(t):
        value = full_term(t, ex)
        for w in (0, 1):
            arrived(rx2.at[t, w], r2_recv.at[t, w])
            value += rx2[t, w].astype(F32)
        ty[t] = value.astype(BF)
        for d in (1, 3, 2):
            to = (ey + d) % LY
            send(
                ty.at[t, rows(to * TOK, TOK)], ry.at[t, d - 1], ry_send.at[t, d - 1], ry_recv.at[t, d - 1],
                owner(ex, to, q), z,
            )

    def home_copy(t, j):
        return remote(tz.at[t, j], rz.at[q, z], rz_send.at[t, j], rz_recv.at[0], e * Q + 2 + t, j)

    def is_here(t, j):
        return jnp.logical_and(q == 2 + t, z == j)

    def plane_home(t):
        value = ty[t, rows(ey * TOK, TOK), :].astype(F32)
        for d in (1, 3, 2):
            arrived(ry.at[t, d - 1], ry_recv.at[t, d - 1])
            value += ry[t, d - 1].astype(F32)
        for j in range(Z):
            tz[t, j] = value[:, j * PIECE : (j + 1) * PIECE].astype(BF)
        for j in range(Z):

            @pl.when(jnp.logical_not(is_here(t, j)))
            def _(j=j):
                home_copy(t, j).start()

            @pl.when(is_here(t, j))
            def _(j=j):
                pltpu.make_async_copy(tz.at[t, j], rz.at[q, z], rz_recv.at[0]).start()

    plane_far(0)
    plane_far(1)
    z_step(0, 0)
    z_step(1, 0)
    plane_near(0)
    z_step(0, 1)
    z_step(1, 1)
    plane_near(1)
    z_step(0, 2)
    plane_y(0)
    z_step(1, 2)
    z_step(0, 3)
    plane_y(1)
    z_step(1, 3)
    plane_home(0)
    z_last(0)
    z_last(1)
    plane_home(1)

    @pl.when(q < 2)
    def _():
        arrived(ret, a_recv.at[0])
        for k in range(Q):
            total = ret[k].astype(F32)
            for x in range(1, EXPERTS):
                total += ret[x * Q + k].astype(F32)
            out[k] = total.astype(BF)
        arrived(ret.at[pl.ds(0, 2 * EXPERTS - 1)], a_send.at[0])

    @pl.when(q >= 2)
    def _():
        arrived(rz, rz_recv.at[0])
        for k in range(Q):
            total = rz[k, 0].astype(F32)
            for j in range(1, Z):
                total += rz[k, j].astype(F32)
            out[k] = total.astype(BF)
        arrived(ret.at[pl.ds(0, 2 * EXPERTS)], a_send.at[0])

    for copy in open_sends:
        copy.wait_send()

    @pl.when(shares)
    def _():
        for copy in g_copies:
            copy.wait_send()

    def factors_sent(i, carry):
        to = (e + i) % EXPERTS * Q + share_of_column

        @pl.when(to != p)
        def _():
            remote(fmat, wbuf.at[q, ey], f_send.at[i], f_recv.at[0], to, z).wait_send()

        return carry

    lax.fori_loop(0, EXPERTS, factors_sent, 0)
    for g in range(2):
        for w in range(2):
            for s in range(4):
                for part in range(2):
                    if s > 0 or part == w:
                        z_copy(g, w, s, part).wait_send()
    for t in range(2):
        for j in range(Z):

            @pl.when(jnp.logical_not(is_here(t, j)))
            def _(t=t, j=j):
                home_copy(t, j).wait_send()


def local(tokens, routes, route_weights, gate_weight, up_weight, down_weight):
    dma = pltpu.SemaphoreType.DMA
    vmem = pl.BlockSpec(memory_space=pltpu.VMEM)
    anywhere = pl.BlockSpec(memory_space=pl.ANY)
    got = pl.pallas_call(
        kernel,
        out_shape=jax.ShapeDtypeStruct((Q, TOK, PIECE), BF),
        in_specs=[anywhere] * 6,
        out_specs=vmem,
        scratch_shapes=[
            pltpu.VMEM((TOK, D), BF),
            pltpu.VMEM((TOP, TOK), jnp.int32),
            pltpu.VMEM((TOP, TOK), F32),
            pltpu.VMEM((Z, ROWS, PART), BF),
            pltpu.VMEM((Q, ROWS, REST), BF),
            pltpu.VMEM((W, UNITS), BF),
            pltpu.VMEM((W, UNITS), BF),
            pltpu.VMEM((UNITS, W), BF),
            pltpu.VMEM((Z, UNITS, PIECE), BF),
            pltpu.VMEM((Q, ROWS, 2 * UNITS), F32),
            pltpu.VMEM((Q, 2 * SHARE, 2 * UNITS), BF),
            pltpu.VMEM((Q, 2 * SHARE, 2 * UNITS), BF),
            pltpu.VMEM((Q, SHARE, 2 * UNITS), BF),
            pltpu.VMEM((Q, SHARE, 2 * UNITS), BF),
            pltpu.VMEM((Q, ROWS, UNITS), BF),
            pltpu.VMEM((TOK, 128), F32),
            pltpu.VMEM((Q, LY, TOK, 128), F32),
            pltpu.VMEM((2, 2, 4, ROWS, PIECE), BF),
            pltpu.VMEM((2, 2, 4, ROWS, PIECE), BF),
            pltpu.VMEM((2, ROWS, PIECE), BF),
            pltpu.VMEM((EXPERTS * Q, TOK, PIECE), BF),
            pltpu.VMEM((2, SHARE, W), BF),
            pltpu.VMEM((2, 2, SHARE // 2, W), BF),
            pltpu.VMEM((2, 2, SHARE, W), BF),
            pltpu.VMEM((2, 2, SHARE, W), BF),
            pltpu.VMEM((2, SHARE, W), BF),
            pltpu.VMEM((2, LY - 1, TOK, W), BF),
            pltpu.VMEM((2, Z, TOK, PIECE), BF),
            pltpu.VMEM((Q, Z, TOK, PIECE), BF),
            dma((6,)), dma((16,)), dma((1,)), dma((4,)), dma((4,)), dma((4,)), dma((4,)),
            dma((4, 4)), dma((4, 4)), dma((4, 4)), dma((4, 4)),
            dma((7,)), dma((7,)), dma((7,)), dma((7,)),
            dma((4,)), dma((4,)), dma((4,)), dma((4,)), dma((4, 4)), dma((4, 4)),
            dma((2, 2, 4, 2)), dma((2, 2, 4, 2)), dma((1,)), dma((1,)),
            dma((16,)), dma((1,)), dma((2, 2)), dma((2, 2)), dma((2, 2)), dma((2, 2)),
            dma((2, 3)), dma((2, 3)), dma((2, 8)), dma((1,)),
        ],
        compiler_params=pltpu.CompilerParams(
            collective_id=0, has_side_effects=True, vmem_limit_bytes=60 * 1024 * 1024
        ),
        cost_estimate=pl.CostEstimate(flops=3 * 10**9, bytes_accessed=4 * 10**6, transcendentals=10**5),
    )(tokens, routes.T, route_weights.T, gate_weight[0], up_weight[0], down_weight[0])
    return got.transpose(1, 0, 2).reshape(TOK, Q * PIECE)


def solution(mesh):
    placed = (
        P("expert", None),
        P("expert", None),
        P("expert", None),
        P("expert", None, "hsplit"),
        P("expert", None, "hsplit"),
        P("expert", "hsplit", None),
    )
    return jax.shard_map(
        local, mesh=mesh, in_specs=placed, out_specs=P("expert", "hsplit"), check_vma=False
    )
```
